256 devices in a mesh: seq: 32 (over y_hi, z, core), tp: 8 (over x, y_lo).
Axes of the slice: x: 4, y: 4 (y_hi: 2, y_lo: 2; y = y_hi * 2 + y_lo), z: 8, core: 2. Of those that a mesh axis runs over, the one named last changes fastest.
Arguments:
- hidden: bfloat16 [4096, 7168], P('seq', 'tp'), may hold values from -6 to 6
- w_kv_down: bfloat16 [7168, 576], P('tp'), may hold values from -0.0625 to 0.0625
- kv_gain: float32 [512], replicated, may hold values from 0.1 to 1.9
- q_latent: bfloat16 [4096, 64, 512], P('seq', 'tp'), may hold values from -300 to 300
- q_rope: bfloat16 [4096, 4096], P('seq', 'tp'), may hold values from -6 to 6
- w_value: bfloat16 [64, 512, 128], P('tp'), may hold values from -0.75 to 0.75
Outputs:
- attended: bfloat16 [4096, 8192], P('seq', 'tp')
The draws below stay inside these ranges and needn't reach their ends.
All inputs are finite; a program needn't handle non-finite values.
Results may differ from the reference program's by a relative error of at most 0.0097.
Values may be sent and summed in bfloat16 or wider, within the bound.
A program may use at most 64 MiB of HBM per device.

```python
import jax
import jax.numpy as jnp
from jax import lax

D = 7168
KV_RANK = 512
ROPE = 64
V_DIM = 128
HEADS = 64
TOKENS = 4096


def draw_q_latent(key, part):
    base = jnp.clip(jax.random.normal(key, (TOKENS, HEADS, KV_RANK), jnp.float32), -4.0, 4.0)
    return base.astype(jnp.bfloat16)


def block_levels(key, dims, split, least, high):
    def one(position, blocks):
        steps = jax.random.uniform(jax.random.fold_in(jax.random.fold_in(key, 6), position), (blocks,), jnp.float32, least / len(split), high / len(split))
        return jnp.repeat(jnp.exp(steps), dims[position] // blocks).reshape((-1,) + (1,) * (len(dims) - position - 1))

    level = one(*split[0])
    for cut in split[1:]:
        level = level * one(*cut)
    return level


def normal_values(key, extent, spread, reach, shards=(), kind=jnp.bfloat16):
    factor_of = block_levels(key, extent, shards, -0.22, 0.18) if shards else 1.0
    entries = jax.random.normal(key, extent, jnp.float32) * spread * factor_of
    return jnp.minimum(jnp.maximum(entries, -reach), reach).astype(kind)


def setup_inputs(seed: int = 0) -> dict:
    arg_keys = jax.random.split(jax.random.key(seed), 7)
    hidden = normal_values(arg_keys[0], (TOKENS, D), 1.0, 6.0, ((0, 32), (1, 8)))
    w_kv_down = normal_values(arg_keys[1], (D, KV_RANK + ROPE), D ** -0.5, 0.0625, ((0, 8),))
    kv_gain = jnp.clip(1.0 + 0.18 * jax.random.normal(arg_keys[2], (KV_RANK,), jnp.float32), 0.1, 1.9)
    q_latent = draw_q_latent(jax.random.fold_in(arg_keys[6], 71), 0)
    q_rope = normal_values(arg_keys[4], (TOKENS, HEADS * ROPE), 1.0, 6.0, ((0, 32), (1, 8)))
    w_value = normal_values(arg_keys[5], (HEADS, KV_RANK, V_DIM), (KV_RANK // 8) ** -0.5, 0.75, ((0, 8),))
    return {"hidden": hidden, "w_kv_down": w_kv_down, "kv_gain": kv_gain, "q_latent": q_latent, "q_rope": q_rope, "w_value": w_value}


SCORE_SCALE = 192.0 ** (-0.5)
ROPE_BASE = 10000.0
EPSILON = 1e-06

def rotate(values, positions):
    full_width = values.shape[-1]
    half_width = full_width // 2
    frequency = ROPE_BASE ** (-jnp.arange(half_width, dtype=jnp.float32) * 2.0 / full_width)
    angles = positions.astype(jnp.float32)[:, None] * frequency[None, :]
    angle_shape = (angles.shape[0],) + (1,) * (values.ndim - 2) + (half_width,)
    cosine = jnp.cos(angles).reshape(angle_shape)
    sine_part = jnp.sin(angles).reshape(angle_shape)
    first_half = values[..., :half_width]
    second_half = values[..., half_width:]
    return jnp.concatenate([first_half * cosine - second_half * sine_part, first_half * sine_part + second_half * cosine], -1)

def finish(projection, kv_gain, positions):
    latent_part = projection[:, :KV_RANK]
    mean_square = lax.optimization_barrier(jnp.mean(latent_part * latent_part, axis=-1, keepdims=True))
    normed = latent_part * lax.rsqrt(mean_square + EPSILON) * kv_gain[None, :]
    rope_part = rotate(projection[:, KV_RANK:], positions)
    return jnp.concatenate([normed, rope_part], -1).astype(jnp.bfloat16)

def reference(hidden, w_kv_down, kv_gain, q_latent, q_rope, w_value):
    positions = jnp.arange(TOKENS, dtype=jnp.int32)
    projection = jnp.dot(hidden, w_kv_down, preferred_element_type=jnp.float32)
    key_rows = lax.optimization_barrier(finish(projection, kv_gain, positions))
    key_float = key_rows.astype(jnp.float32)
    rope_query = rotate(q_rope.astype(jnp.float32).reshape(TOKENS, HEADS, ROPE), positions).astype(jnp.bfloat16)
    rope_query = lax.optimization_barrier(rope_query)
    queries = jnp.concatenate([q_latent, rope_query], -1)
    block_rows = min(256, TOKENS)
    block_count = TOKENS // block_rows

    def attend_block(block_index):
        first_row = block_index * block_rows
        query_rows = lax.dynamic_slice_in_dim(queries, first_row, block_rows, 0).astype(jnp.float32)
        scores = jnp.einsum('qhc,kc->hqk', query_rows, key_float) * SCORE_SCALE
        query_positions = first_row + jnp.arange(block_rows, dtype=jnp.int32)
        allowed = (positions[None, :] <= query_positions[:, None])[None]
        scores = jnp.where(allowed, scores, -1e+30)
        row_max = lax.optimization_barrier(jnp.max(scores, axis=-1, keepdims=True))
        weights = jnp.where(allowed, jnp.exp(scores - row_max), 0.0)
        weight_total = lax.optimization_barrier(jnp.sum(weights, axis=-1))
        rounded = lax.optimization_barrier(weights.astype(jnp.bfloat16))
        mixed_keys = jnp.einsum('hqk,kc->hqc', rounded.astype(jnp.float32), key_float[:, :KV_RANK])
        latent_out = lax.optimization_barrier((mixed_keys / weight_total[..., None]).astype(jnp.bfloat16))
        projected = jnp.einsum('hqc,hcv->qhv', latent_out.astype(jnp.float32), w_value.astype(jnp.float32))
        return projected.astype(jnp.bfloat16).reshape(block_rows, HEADS * V_DIM)
    results = lax.map(attend_block, jnp.arange(block_count, dtype=jnp.int32))
    return results.reshape(TOKENS, HEADS * V_DIM)
```

```python
import jax
import jax.numpy as jnp
import numpy as np
from jax import lax
from jax.experimental import pallas as pl
from jax.experimental.pallas import tpu as pltpu
from jax.sharding import PartitionSpec as P

MESH = pl.DeviceIdType.MESH
KV_RANK = 512
ROPE = 64
WIDTH = KV_RANK + ROPE
V_DIM = 128
TOK = 128
HEADS = 8
ROWS = TOK * HEADS
TP = 8
SLICE = TOK // TP
UNIT = 8 * SLICE
BLOCK = 4 * UNIT
EPSILON = 1e-06
LOG2E = 1.4426950408889634
EXP_SCALE = 192.0 ** (-0.5) * LOG2E
NT = (((1,), (1,)), ((), ()))
NN = (((1,), (0,)), ((), ()))
TN = (((0,), (0,)), ((), ()))


def dot(a, b, dims):
    return lax.dot_general(a, b, dims, preferred_element_type=jnp.float32)


def kernel(
    hidden, w_down, gain, q_latent, q_rope, w_value, freq, out,
    hid_v, wd_v, ql_v, qr_v, wv_v, partial, sums, keys, q_f32, queries, cos_t, sin_t, acc, top, total,
    load_sem, rs_s, rs_r, z_s, z_r, a_s, a_r, b_s, b_r, f_s, f_r, c_s, c_r,
):
    seq = lax.axis_index("seq")
    tp = lax.axis_index("tp")
    core = seq % 2
    z = (seq // 2) % 8
    y_hi = seq // 16
    x = tp // 2
    y_lo = tp % 2
    y = y_hi * 2 + y_lo

    def device(x_, y_, z_):
        return (((y_ // 2) * 8 + z_) * 2 + core, x_ * 2 + y_ % 2)

    a_me = x * (1 - core) + y * core
    b_me = y * (1 - core) + x * core

    def plane(a_, b_):
        return device(a_ * (1 - core) + b_ * core, b_ * (1 - core) + a_ * core, z)

    sibling = (seq + 1 - 2 * core, tp)

    loads = [
        pltpu.make_async_copy(src, dst, load_sem.at[i])
        for i, (src, dst) in enumerate(
            ((hidden, hid_v), (w_down, wd_v), (q_rope, qr_v), (q_latent, ql_v), (w_value, wv_v))
        )
    ]
    for load in loads:
        load.start()

    barrier = pltpu.get_barrier_semaphore()
    peers = [(seq, (tp + d) % TP) for d in range(1, TP)]
    peers += [device(x, y, (z + d) % 8) for d in range(1, 8)]
    peers += [sibling, device(x, 3 - y, z), device(x, (y + 2) % 4, z)]
    for peer in peers:
        pl.semaphore_signal(barrier, inc=1, device_id=peer, device_id_type=MESH)

    loads[0].wait()
    loads[1].wait()
    partial[...] = dot(hid_v[...], wd_v[...], NN)
    pl.semaphore_wait(barrier, len(peers))

    sent = []

    def copy(src, dst, send_sem, recv_sem, target):
        return pltpu.make_async_remote_copy(
            src_ref=src, dst_ref=dst, send_sem=send_sem, recv_sem=recv_sem, device_id=target, device_id_type=MESH
        )

    def start(*args):
        one = copy(*args)
        one.start()
        sent.append(one)

    def rows_of(owner):
        return partial.at[pl.ds(pl.multiple_of(owner * SLICE, SLICE), SLICE), :]

    for d in range(1, TP):
        owner = (tp + d) % TP
        start(rows_of(owner), sums.at[d], rs_s.at[d], rs_r.at[d], (seq, owner))

    positions = (seq * TOK + lax.broadcasted_iota(jnp.int32, (TOK, 128), 0)).astype(jnp.float32)
    angles = positions * freq[...]
    lane = lax.broadcasted_iota(jnp.int32, (1, 128), 1)
    cos_t[...] = jnp.cos(angles)
    sin_t[...] = jnp.where(lane % ROPE < ROPE // 2, -jnp.sin(angles), jnp.sin(angles))
    loads[2].wait()
    raw = qr_v[...].astype(jnp.float32)
    wide_lane = lax.broadcasted_iota(jnp.int32, (1, HEADS * ROPE), 1)
    swapped = jnp.where(
        wide_lane % ROPE < ROPE // 2,
        pltpu.roll(raw, HEADS * ROPE - ROPE // 2, 1),
        pltpu.roll(raw, ROPE // 2, 1),
    )
    repeat = HEADS * ROPE // 128
    rotated = raw * jnp.concatenate([cos_t[...]] * repeat, 1) + swapped * jnp.concatenate([sin_t[...]] * repeat, 1)
    rotated = rotated.astype(jnp.bfloat16)
    loads[3].wait()
    for c in range(KV_RANK // 128):
        q_f32[c] = ql_v[:, c * 128:(c + 1) * 128].astype(jnp.float32)
    for h in range(HEADS):
        for c in range(KV_RANK // 128):
            queries[h * TOK:(h + 1) * TOK, c * 128:(c + 1) * 128] = q_f32[
                c, pl.ds(h, TOK, stride=HEADS), :
            ].astype(jnp.bfloat16)
        queries[h * TOK:(h + 1) * TOK, KV_RANK:] = rotated[:, h * ROPE:(h + 1) * ROPE]

    for d in range(1, TP):
        copy(rows_of(tp), sums.at[d], rs_s.at[d], rs_r.at[d], (seq, tp)).wait_recv()
    mine = pl.ds(pl.multiple_of(tp * SLICE, SLICE), SLICE)
    projection = partial[mine, :]
    for d in range(1, TP):
        projection = projection + sums[d]
    latent = projection[:, :KV_RANK]
    mean_square = jnp.mean(latent * latent, axis=-1, keepdims=True)
    latent = latent * lax.rsqrt(mean_square + EPSILON) * gain[...]
    rope = projection[:, KV_RANK:]
    rope_swapped = jnp.concatenate([rope[:, ROPE // 2:], rope[:, :ROPE // 2]], 1)
    rope = rope * cos_t[mine, :ROPE] + rope_swapped * sin_t[mine, :ROPE]

    def unit(which, a_, b_):
        return keys.at[which, pl.ds(pl.multiple_of((b_ * 4 + a_) * UNIT, UNIT), UNIT), :]

    def slot(z_):
        return keys.at[core, pl.ds(pl.multiple_of(((b_me * 4 + a_me) * 8 + z_) * SLICE, SLICE), SLICE), :]

    slot(z)[...] = jnp.concatenate([latent, rope], 1).astype(jnp.bfloat16)

    for d in (4, 3, 5, 2, 6, 1, 7):
        start(slot(z), slot(z), z_s.at[d], z_r.at[d], device(x, y, (z + d) % 8))
    for d in range(1, 8):
        there = slot((z - d) % 8)
        copy(there, there, z_s.at[d], z_r.at[d], sibling).wait_recv()

    def to_sibling(i, a_, b_):
        here = unit(core, a_, b_)
        start(here, here, c_s.at[i], c_r.at[i], sibling)

    def to_b(i, a_):
        here = unit(core, a_, b_me)
        start(here, here, b_s.at[0, i], b_r.at[0, i], plane(a_me, (b_me + 1) % 4))
        start(here, here, b_s.at[1, i], b_r.at[1, i], plane(a_me, (b_me + 3) % 4))

    order = (0, 1, 3, 2)
    own = unit(core, a_me, b_me)
    for d in (2, 1, 3):
        start(own, own, a_s.at[d], a_r.at[d], plane((a_me + d) % 4, b_me))
    to_b(0, a_me)
    to_sibling(0, a_me, b_me)
    for i, d in enumerate(order[1:], 1):
        a_ = (a_me + 4 - d) % 4
        there = unit(core, a_, b_me)
        copy(there, there, a_s.at[d], a_r.at[d], sibling).wait_recv()
        to_b(i, a_)
        to_sibling(i, a_, b_me)

    def from_sibling(group, b_there):
        for i, d in enumerate(order):
            there = unit(1 - core, (b_me + 4 - d) % 4, b_there)
            copy(there, there, c_s.at[group * 4 + i], c_r.at[group * 4 + i], sibling).wait_recv()

    query_pos = seq * TOK + lax.broadcasted_iota(jnp.int32, (1, TOK), 1)

    def block_scores(which, b_):
        index = lax.broadcasted_iota(jnp.int32, (BLOCK, TOK), 0)
        a_i = index // UNIT
        z_i = (index // SLICE) % 8
        x_i = a_i * (1 - which) + b_ * which
        y_i = b_ * (1 - which) + a_i * which
        key_pos = (((y_i // 2) * 8 + z_i) * 2 + which) * TOK + (x_i * 2 + y_i % 2) * SLICE + index % SLICE
        bias = jnp.where(key_pos <= query_pos, 0.0, -1e30)
        rows = keys[which, pl.ds(pl.multiple_of(b_ * BLOCK, BLOCK), BLOCK), :]
        scores = dot(rows, queries[...], NT) + jnp.concatenate([bias] * HEADS, 1)
        return rows, scores

    def attend(b_own, b_other, first):
        rows_0, scores_0 = block_scores(core, b_own)
        rows_1, scores_1 = block_scores(1 - core, b_other)
        here = jnp.maximum(jnp.max(scores_0, 0, keepdims=True), jnp.max(scores_1, 0, keepdims=True))
        new_top = here if first else jnp.maximum(top[0:1, :], here)
        shift = new_top * EXP_SCALE
        weights_0 = jnp.exp2(scores_0 * EXP_SCALE - shift)
        weights_1 = jnp.exp2(scores_1 * EXP_SCALE - shift)
        added = jnp.sum(weights_0, 0, keepdims=True) + jnp.sum(weights_1, 0, keepdims=True)
        mixed = dot(rows_0[:, :KV_RANK], weights_0.astype(jnp.bfloat16), TN) + dot(
            rows_1[:, :KV_RANK], weights_1.astype(jnp.bfloat16), TN
        )
        if first:
            total[0:1, :] = added
            acc[...] = mixed
        else:
            scale = jnp.exp2(top[0:1, :] * EXP_SCALE - shift)
            total[0:1, :] = total[0:1, :] * scale + added
            acc[...] = acc[...] * scale + mixed
        top[0:1, :] = new_top

    b_less, b_more, b_far = (b_me + 3) % 4, (b_me + 1) % 4, (b_me + 2) % 4
    a_less, a_more, a_far = (a_me + 3) % 4, (a_me + 1) % 4, (a_me + 2) % 4

    from_sibling(0, a_me)
    attend(b_me, a_me, True)

    for i, d in enumerate(order):
        a_ = (a_me + 4 - d) % 4
        there = unit(core, a_, b_less)
        copy(there, there, b_s.at[0, i], b_r.at[0, i], sibling).wait_recv()
        if i < 2:
            start(there, there, f_s.at[i], f_r.at[i], plane(a_me, b_more))
        to_sibling(4 + i, a_, b_less)
    for i, d in enumerate(order):
        a_ = (a_me + 4 - d) % 4
        there = unit(core, a_, b_more)
        copy(there, there, b_s.at[1, i], b_r.at[1, i], sibling).wait_recv()
        if i >= 2:
            start(there, there, f_s.at[i], f_r.at[i], plane(a_me, b_less))
        to_sibling(8 + i, a_, b_more)

    from_sibling(1, a_less)
    attend(b_less, a_less, False)
    from_sibling(2, a_more)
    attend(b_more, a_more, False)
    for i, d in enumerate(order):
        a_ = (a_me + 4 - d) % 4
        there = unit(core, a_, b_far)
        copy(there, there, f_s.at[i], f_r.at[i], sibling).wait_recv()
        to_sibling(12 + i, a_, b_far)
    from_sibling(3, a_far)
    attend(b_far, a_far, False)

    loads[4].wait()
    mixed = (acc[...] / total[0:1, :]).astype(jnp.bfloat16)
    for h in range(HEADS):
        cut = slice(h * TOK, (h + 1) * TOK)
        out[:, h * V_DIM:(h + 1) * V_DIM] = dot(mixed[:, cut], wv_v[h], TN).astype(jnp.bfloat16)
    for one in sent:
        one.wait_send()


def shards(hidden, w_kv_down, kv_gain, q_latent, q_rope, w_value):
    half = ROPE // 2
    frequency = (10000.0 ** (-np.arange(half, dtype=np.float64) * 2.0 / ROPE)).astype(np.float32)
    freq = jnp.asarray(np.tile(frequency, 4)[None, :])
    hbm = pl.BlockSpec(memory_space=pl.ANY)
    vmem = pl.BlockSpec(memory_space=pltpu.VMEM)
    bf16, f32 = jnp.bfloat16, jnp.float32
    dma = pltpu.SemaphoreType.DMA
    width = hidden.shape[1]
    return pl.pallas_call(
        kernel,
        name="latent_attention",
        out_shape=jax.ShapeDtypeStruct((TOK, HEADS * V_DIM), bf16),
        in_specs=[hbm, hbm, vmem, hbm, hbm, hbm, vmem],
        out_specs=vmem,
        scratch_shapes=[
            pltpu.VMEM((TOK, width), bf16),
            pltpu.VMEM((width, WIDTH), bf16),
            pltpu.VMEM((ROWS, KV_RANK), bf16),
            pltpu.VMEM((TOK, HEADS * ROPE), bf16),
            pltpu.VMEM((HEADS, KV_RANK, V_DIM), bf16),
            pltpu.VMEM((TOK, WIDTH), f32),
            pltpu.VMEM((TP, SLICE, WIDTH), f32),
            pltpu.VMEM((2, 4 * BLOCK, WIDTH), bf16),
            pltpu.VMEM((KV_RANK // 128, ROWS, 128), f32),
            pltpu.VMEM((ROWS, WIDTH), bf16),
            pltpu.VMEM((TOK, 128), f32),
            pltpu.VMEM((TOK, 128), f32),
            pltpu.VMEM((KV_RANK, ROWS), f32),
            pltpu.VMEM((8, ROWS), f32),
            pltpu.VMEM((8, ROWS), f32),
            dma((5,)),
            dma((8,)), dma((8,)),
            dma((8,)), dma((8,)),
            dma((4,)), dma((4,)),
            dma((2, 4)), dma((2, 4)),
            dma((4,)), dma((4,)),
            dma((16,)), dma((16,)),
        ],
        compiler_params=pltpu.CompilerParams(
            collective_id=0, has_side_effects=True, vmem_limit_bytes=50 * 2**20
        ),
    )(
        hidden,
        w_kv_down,
        kv_gain[None, :],
        q_latent.reshape(ROWS, KV_RANK),
        q_rope,
        w_value,
        freq,
    )


def solution(mesh):
    placed = (
        P("seq", "tp"),
        P("tp", None),
        P(),
        P("seq", "tp", None),
        P("seq", "tp"),
        P("tp", None, None),
    )
    return jax.shard_map(
        shards, mesh=mesh, in_specs=placed, out_specs=P("seq", "tp"), check_vma=False
    )
```

```python
import functools

import jax
import jax.numpy as jnp
import numpy as np
from jax import lax
from jax.experimental import pallas as pl
from jax.experimental.pallas import tpu as pltpu
from jax.sharding import PartitionSpec as P

MESH = pl.DeviceIdType.MESH
KV_RANK = 512
ROPE = 64
WIDTH = KV_RANK + ROPE
V_DIM = 128
TOK = 128
HEADS = 8
ROWS = TOK * HEADS
TP = 8
SLICE = TOK // TP
UNIT = 8 * SLICE
EPSILON = 1e-06
LOG2E = 1.4426950408889634
EXP_SCALE = 192.0 ** (-0.5) * LOG2E
NT = (((1,), (1,)), ((), ()))
TN = (((0,), (0,)), ((), ()))


def dot(a, b, dims):
    return lax.dot_general(a, b, dims, preferred_element_type=jnp.float32)


def maybe(cond, act):
    if cond is True:
        act()
    else:
        pl.when(cond)(act)


ME, MATE, CROSS, FAR = range(4)
NEAR = (ME, MATE)


def near(i, label):
    sign = 1 - 2 * (i % 2)
    return (i + (0, sign, 4 - sign, 2)[label]) % 4


def arrange():
    stages = (
        ((ME, ME),),
        ((MATE, ME), (CROSS, ME), (FAR, ME), (ME, MATE), (ME, CROSS)),
        ((CROSS, MATE), (FAR, MATE), (MATE, CROSS), (CROSS, CROSS)),
        ((MATE, MATE), (FAR, CROSS)),
        ((ME, FAR), (CROSS, FAR)),
        ((MATE, FAR), (FAR, FAR)),
    )
    labels = []
    for masked in (True, False):
        for stage in stages:
            for lineage in range(2):
                labels += [(lineage, a, b) for a, b in stage if ((b, a)[lineage] in NEAR) == masked]
    return labels


LABELS = arrange()
PLACE = {label: place for place, label in enumerate(LABELS)}


def kernel(
    hidden, w_down, gain, q_latent, q_rope, w_value, freq, out,
    hid_v, wd_v, ql_v, qr_v, wv_v, partial, sums, keys, q_f32, queries, cos_t, sin_t, acc, top, total,
    load_sem, rs_s, rs_r, z_s, z_r, a_s, a_r, b_s, b_r, f_s, f_r, c_s, c_r,
):
    seq = lax.axis_index("seq")
    tp = lax.axis_index("tp")
    core = seq % 2
    z = (seq // 2) % 8
    y_hi = seq // 16
    x = tp // 2
    y_lo = tp % 2
    y = y_hi * 2 + y_lo

    def device(x_, y_, z_):
        return (((y_ // 2) * 8 + z_) * 2 + core, x_ * 2 + y_ % 2)

    a_me = x * (1 - core) + y * core
    b_me = y * (1 - core) + x * core

    def plane(a_, b_):
        return device(a_ * (1 - core) + b_ * core, b_ * (1 - core) + a_ * core, z)

    sibling = (seq + 1 - 2 * core, tp)

    loads = [
        pltpu.make_async_copy(src, dst, load_sem.at[i])
        for i, (src, dst) in enumerate(
            ((hidden, hid_v), (w_down, wd_v), (q_rope, qr_v), (q_latent, ql_v), (w_value, wv_v))
        )
    ]
    for load in loads:
        load.start()

    barrier = pltpu.get_barrier_semaphore()
    peers = [(seq, (tp + d) % TP) for d in range(1, TP)]
    peers += [device(x, y, (z + d) % 8) for d in range(1, 8)]
    peers += [sibling, device(x, 3 - y, z), device(x, (y + 2) % 4, z)]
    for peer in peers:
        pl.semaphore_signal(barrier, inc=1, device_id=peer, device_id_type=MESH)

    loads[0].wait()
    loads[1].wait()
    partial[...] = dot(hid_v[...], wd_v[...], NT)
    pl.semaphore_wait(barrier, len(peers))

    sent = []

    def copy(src, dst, send_sem, recv_sem, target):
        return pltpu.make_async_remote_copy(
            src_ref=src, dst_ref=dst, send_sem=send_sem, recv_sem=recv_sem, device_id=target, device_id_type=MESH
        )

    def start(cond, *args):
        one = copy(*args)
        maybe(cond, one.start)
        sent.append((cond, one))

    def rows_of(owner):
        return partial.at[pl.ds(pl.multiple_of(owner * SLICE, SLICE), SLICE), :]

    for d in range(1, TP):
        owner = (tp + d) % TP
        start(True, rows_of(owner), sums.at[d], rs_s.at[d], rs_r.at[d], (seq, owner))

    positions = (seq * TOK + lax.broadcasted_iota(jnp.int32, (TOK, 128), 0)).astype(jnp.float32)
    angles = positions * freq[...]
    lane = lax.broadcasted_iota(jnp.int32, (1, 128), 1)
    cos_t[...] = jnp.cos(angles)
    sin_t[...] = jnp.where(lane % ROPE < ROPE // 2, -jnp.sin(angles), jnp.sin(angles))
    loads[2].wait()
    raw = qr_v[...].astype(jnp.float32)
    wide_lane = lax.broadcasted_iota(jnp.int32, (1, HEADS * ROPE), 1)
    swapped = jnp.where(
        wide_lane % ROPE < ROPE // 2,
        pltpu.roll(raw, HEADS * ROPE - ROPE // 2, 1),
        pltpu.roll(raw, ROPE // 2, 1),
    )
    repeat = HEADS * ROPE // 128
    rotated = raw * jnp.concatenate([cos_t[...]] * repeat, 1) + swapped * jnp.concatenate([sin_t[...]] * repeat, 1)
    rotated = rotated.astype(jnp.bfloat16)
    loads[3].wait()
    for c in range(KV_RANK // 128):
        q_f32[c] = ql_v[:, c * 128:(c + 1) * 128].astype(jnp.float32)
    for h in range(HEADS):
        for c in range(KV_RANK // 128):
            queries[h * TOK:(h + 1) * TOK, c * 128:(c + 1) * 128] = q_f32[
                c, pl.ds(h, TOK, stride=HEADS), :
            ].astype(jnp.bfloat16)
        queries[h * TOK:(h + 1) * TOK, KV_RANK:] = rotated[:, h * ROPE:(h + 1) * ROPE]

    for d in range(1, TP):
        copy(rows_of(tp), sums.at[d], rs_s.at[d], rs_r.at[d], (seq, tp)).wait_recv()
    mine = pl.ds(pl.multiple_of(tp * SLICE, SLICE), SLICE)
    projection = partial[mine, :]
    for d in range(1, TP):
        projection = projection + sums[d]
    latent = projection[:, :KV_RANK]
    mean_square = jnp.mean(latent * latent, axis=-1, keepdims=True)
    latent = latent * lax.rsqrt(mean_square + EPSILON) * gain[...]
    rope = projection[:, KV_RANK:]
    rope_swapped = jnp.concatenate([rope[:, ROPE // 2:], rope[:, :ROPE // 2]], 1)
    rope = rope * cos_t[mine, :ROPE] + rope_swapped * sin_t[mine, :ROPE]

    def unit_at(lineage, a, b):
        first, second = PLACE[0, a, b], PLACE[1, a, b]
        place = first + (second - first) * lineage
        return keys.at[pl.ds(pl.multiple_of(place * UNIT, UNIT), UNIT), :]

    def unit(a, b):
        return unit_at(core, a, b)

    own_place = PLACE[0, ME, ME] + (PLACE[1, ME, ME] - PLACE[0, ME, ME]) * core

    def slot(z_):
        return keys.at[pl.ds(pl.multiple_of(own_place * UNIT + z_ * SLICE, SLICE), SLICE), :]

    slot(z)[...] = jnp.concatenate([latent, rope], 1).astype(jnp.bfloat16)

    for d in (4, 3, 5, 2, 6, 1, 7):
        start(True, slot(z), slot(z), z_s.at[d], z_r.at[d], device(x, y, (z + d) % 8))
    for d in range(1, 8):
        there = slot((z - d) % 8)
        copy(there, there, z_s.at[d], z_r.at[d], sibling).wait_recv()

    early, late, even, odd = y_hi == 0, y_hi == 1, core == 0, core == 1

    def needed(lineage_even, a, b):
        if a in NEAR and b in NEAR:
            return True
        if b in NEAR:
            return late | lineage_even
        if a in NEAR:
            return late | jnp.logical_not(lineage_even)
        return late

    def send_a(a):
        cond = True if a == MATE else even | early
        start(cond, unit(ME, ME), unit(a, ME), a_s.at[a], a_r.at[a], plane(near(a_me, a), b_me))

    def send_b(a, b):
        if b == MATE:
            cond = True if a in NEAR else even | late
        else:
            cond = (even & early) | odd if a in NEAR else (even & early) | (odd & late)
        start(cond, unit(a, ME), unit(a, b), b_s.at[b, a], b_r.at[b, a], plane(a_me, near(b_me, b)))

    def forward(a):
        came, goes = (CROSS, MATE) if a in NEAR else (MATE, CROSS)
        if goes == MATE:
            cond = odd | late
        else:
            cond = (even & early) | (odd & late)
        start(cond, unit(a, came), unit(a, FAR), f_s.at[a], f_r.at[a], plane(a_me, near(b_me, goes)))

    def to_sibling(a, b):
        start(needed(even, a, b), unit(a, b), unit(a, b), c_s.at[b, a], c_r.at[b, a], sibling)

    def arrived(cond, ref, recv_sem):
        maybe(cond, copy(ref, ref, c_s.at[0, 0], recv_sem, sibling).wait_recv)

    def got_a(a):
        arrived(needed(even, a, ME), unit(a, ME), a_r.at[a])

    def got_b(a, b):
        arrived(needed(even, a, b), unit(a, b), b_r.at[b, a])

    def got_far(a):
        arrived(needed(even, a, FAR), unit(a, FAR), f_r.at[a])

    def got_sibling(*labels):
        for a, b in labels:
            arrived(needed(odd, a, b), unit_at(1 - core, a, b), c_r.at[b, a])

    row = lax.broadcasted_iota(jnp.int32, (UNIT, TOK), 0)
    token = lax.broadcasted_iota(jnp.int32, (UNIT, TOK), 1)
    ahead = (row // SLICE) * (2 * TOK) + row % SLICE - token

    def bias(place):
        lineage, a, b = LABELS[place]
        x_label, y_label = (a, b) if lineage == 0 else (b, a)
        base = (lineage - core - 2 * z) * TOK + (near(x, x_label) * 2 + near(y, y_label) % 2) * SLICE
        return jnp.concatenate([jnp.where(ahead + base <= 0, 0.0, -1e30)] * HEADS, 1)

    def attend(masked, free, first=False):
        rows, scores = [], []
        for (begin, end), is_masked in ((masked, True), (free, False)):
            if begin == end:
                continue
            rows.append(keys[begin * UNIT:end * UNIT, :])
            block = dot(rows[-1], queries[...], NT)
            if is_masked:
                block = block + jnp.concatenate([bias(place) for place in range(begin, end)], 0)
            scores.append(block)
        new_top = functools.reduce(jnp.maximum, [jnp.max(block, 0, keepdims=True) for block in scores])
        if not first:
            new_top = jnp.maximum(top[0:1, :], new_top)
        shift = new_top * EXP_SCALE
        added, mixed = 0.0, 0.0
        for keys_here, block in zip(rows, scores):
            weights = jnp.exp2(block * EXP_SCALE - shift)
            added = added + jnp.sum(weights, 0, keepdims=True)
            mixed = mixed + dot(keys_here[:, :KV_RANK], weights.astype(jnp.bfloat16), TN)
        if first:
            total[0:1, :] = added
            acc[...] = mixed
        else:
            scale = jnp.exp2(top[0:1, :] * EXP_SCALE - shift)
            total[0:1, :] = total[0:1, :] * scale + added
            acc[...] = acc[...] * scale + mixed
        top[0:1, :] = new_top

    def chunk(masked_late, free_late, masked_early):
        @pl.when(late)
        def _():
            attend(masked_late, free_late)

        if masked_early is not None:
            @pl.when(early)
            def _():
                attend(masked_early, (0, 0))

    for a in (MATE, CROSS, FAR):
        send_a(a)
    send_b(ME, MATE)
    send_b(ME, CROSS)
    to_sibling(ME, ME)
    got_sibling((ME, ME))
    attend((0, 2), (0, 0), first=True)

    got_a(MATE)
    send_b(MATE, CROSS)
    got_a(CROSS)
    send_b(CROSS, MATE)
    send_b(CROSS, CROSS)
    got_a(FAR)
    send_b(FAR, MATE)
    send_b(FAR, CROSS)
    send_b(MATE, MATE)
    for a in (MATE, CROSS, FAR):
        to_sibling(a, ME)
    got_b(ME, CROSS)
    forward(ME)
    to_sibling(ME, CROSS)
    got_b(ME, MATE)
    to_sibling(ME, MATE)
    got_sibling((MATE, ME), (CROSS, ME), (FAR, ME), (ME, CROSS), (ME, MATE))
    chunk((2, 9), (16, 19), (2, 9))

    got_b(CROSS, MATE)
    forward(CROSS)
    to_sibling(CROSS, MATE)
    got_b(MATE, CROSS)
    forward(MATE)
    to_sibling(MATE, CROSS)
    got_b(FAR, MATE)
    forward(FAR)
    to_sibling(FAR, MATE)
    got_b(CROSS, CROSS)
    to_sibling(CROSS, CROSS)
    got_sibling((CROSS, MATE), (MATE, CROSS), (FAR, MATE), (CROSS, CROSS))
    chunk((9, 12), (19, 24), None)

    got_b(MATE, MATE)
    to_sibling(MATE, MATE)
    got_b(FAR, CROSS)
    to_sibling(FAR, CROSS)
    got_sibling((MATE, MATE), (FAR, CROSS))

    @pl.when(early)
    def _():
        attend((9, 14), (0, 0))

    got_far(ME)
    to_sibling(ME, FAR)
    got_far(CROSS)
    to_sibling(CROSS, FAR)
    got_sibling((ME, FAR), (CROSS, FAR))
    chunk((12, 15), (24, 29), None)

    got_far(MATE)
    to_sibling(MATE, FAR)
    got_far(FAR)
    to_sibling(FAR, FAR)
    got_sibling((MATE, FAR), (FAR, FAR))
    chunk((15, 16), (29, 32), (14, 16))

    loads[4].wait()
    mixed = (acc[...] / total[0:1, :]).astype(jnp.bfloat16)
    for h in range(HEADS):
        cut = slice(h * TOK, (h + 1) * TOK)
        out[:, h * V_DIM:(h + 1) * V_DIM] = dot(mixed[:, cut], wv_v[h], TN).astype(jnp.bfloat16)
    for cond, one in sent:
        maybe(cond, one.wait_send)


def shards(hidden, w_kv_down, kv_gain, q_latent, q_rope, w_value):
    half = ROPE // 2
    frequency = (10000.0 ** (-np.arange(half, dtype=np.float64) * 2.0 / ROPE)).astype(np.float32)
    freq = jnp.asarray(np.tile(frequency, 4)[None, :])
    hbm = pl.BlockSpec(memory_space=pl.ANY)
    vmem = pl.BlockSpec(memory_space=pltpu.VMEM)
    bf16, f32 = jnp.bfloat16, jnp.float32
    dma = pltpu.SemaphoreType.DMA
    width = hidden.shape[1]
    return pl.pallas_call(
        kernel,
        name="latent_attention",
        out_shape=jax.ShapeDtypeStruct((TOK, HEADS * V_DIM), bf16),
        in_specs=[hbm, hbm, vmem, hbm, hbm, hbm, vmem],
        out_specs=vmem,
        scratch_shapes=[
            pltpu.VMEM((TOK, width), bf16),
            pltpu.VMEM((WIDTH, width), bf16),
            pltpu.VMEM((ROWS, KV_RANK), bf16),
            pltpu.VMEM((TOK, HEADS * ROPE), bf16),
            pltpu.VMEM((HEADS, KV_RANK, V_DIM), bf16),
            pltpu.VMEM((TOK, WIDTH), f32),
            pltpu.VMEM((TP, SLICE, WIDTH), f32),
            pltpu.VMEM((32 * UNIT, WIDTH), bf16),
            pltpu.VMEM((KV_RANK // 128, ROWS, 128), f32),
            pltpu.VMEM((ROWS, WIDTH), bf16),
            pltpu.VMEM((TOK, 128), f32),
            pltpu.VMEM((TOK, 128), f32),
            pltpu.VMEM((KV_RANK, ROWS), f32),
            pltpu.VMEM((8, ROWS), f32),
            pltpu.VMEM((8, ROWS), f32),
            dma((5,)),
            dma((8,)), dma((8,)),
            dma((8,)), dma((8,)),
            dma((4,)), dma((4,)),
            dma((4, 4)), dma((4, 4)),
            dma((4,)), dma((4,)),
            dma((4, 4)), dma((4, 4)),
        ],
        compiler_params=pltpu.CompilerParams(
            collective_id=0, has_side_effects=True, vmem_limit_bytes=60 * 2**20
        ),
    )(
        hidden,
        w_kv_down.T,
        kv_gain[None, :],
        q_latent.reshape(ROWS, KV_RANK),
        q_rope,
        w_value,
        freq,
    )


def solution(mesh):
    placed = (
        P("seq", "tp"),
        P("tp", None),
        P(),
        P("seq", "tp", None),
        P("seq", "tp"),
        P("tp", None, None),
    )
    return jax.shard_map(
        shards, mesh=mesh, in_specs=placed, out_specs=P("seq", "tp"), check_vma=False
    )
```

```python
import functools

import jax
import jax.numpy as jnp
import numpy as np
from jax import lax
from jax.experimental import pallas as pl
from jax.experimental.pallas import tpu as pltpu
from jax.sharding import PartitionSpec as P

MESH = pl.DeviceIdType.MESH
KV_RANK = 512
ROPE = 64
WIDTH = KV_RANK + ROPE
V_DIM = 128
TOK = 128
HEADS = 8
HALF = 64
ROWS = TOK * HEADS
TP = 8
SLICE = TOK // TP
EPSILON = 1e-06
LOG2E = 1.4426950408889634
EXP_SCALE = 192.0 ** (-0.5) * LOG2E
NT = (((1,), (1,)), ((), ()))
TN = (((0,), (0,)), ((), ()))


def dot(a, b, dims):
    return lax.dot_general(a, b, dims, preferred_element_type=jnp.float32)


def maybe(cond, act):
    if cond is True:
        act()
    else:
        pl.when(cond)(act)


ME, MATE, CROSS, FAR = range(4)
NEAR = (ME, MATE)


def near(i, label):
    sign = 1 - 2 * (i % 2)
    return (i + (0, sign, 4 - sign, 2)[label]) % 4


def is_masked(lineage, a, b):
    return (b, a)[lineage] in NEAR


def arrange():
    stages = (
        ((ME, ME),),
        ((MATE, ME), (CROSS, ME), (FAR, ME)),
        ((ME, MATE), (ME, CROSS), (ME, FAR)),
        ((MATE, MATE), (MATE, CROSS), (MATE, FAR)),
        ((CROSS, MATE), (CROSS, CROSS), (CROSS, FAR)),
        ((FAR, MATE), (FAR, CROSS), (FAR, FAR)),
    )
    labels, bounds = [], []
    for stage in stages:
        both = [(lineage, a, b) for lineage in range(2) for a, b in stage]
        free = [(*label, part) for label in both if not is_masked(*label) for part in range(2)]
        masked = [(*label, part) for part in range(2) for label in both if is_masked(*label)]
        start = len(labels)
        labels += free + masked
        bounds.append((start, start + len(free), start + len(free) + len(masked) // 2, len(labels)))
    return labels, bounds


LABELS, BOUNDS = arrange()
PLACE = {label: place for place, label in enumerate(LABELS)}


def kernel(
    hidden, w_down, gain, q_latent, q_rope, w_value, freq, out,
    hid_v, wd_v, ql_v, qr_v, wv_v, partial, sums, keys, q_f32, queries, cos_t, sin_t, acc, top, total,
    load_sem, rs_s, rs_r, z_s, z_r, a_s, a_r, b_s, b_r, c_s, c_r,
):
    seq = lax.axis_index("seq")
    tp = lax.axis_index("tp")
    core = seq % 2
    z = (seq // 2) % 8
    y_hi = seq // 16
    x = tp // 2
    y_lo = tp % 2
    y = y_hi * 2 + y_lo

    def device(x_, y_, z_):
        return (((y_ // 2) * 8 + z_) * 2 + core, x_ * 2 + y_ % 2)

    a_me = x * (1 - core) + y * core
    b_me = y * (1 - core) + x * core

    def plane(a_, b_):
        return device(a_ * (1 - core) + b_ * core, b_ * (1 - core) + a_ * core, z)

    sibling = (seq + 1 - 2 * core, tp)

    loads = [
        pltpu.make_async_copy(src, dst, load_sem.at[i])
        for i, (src, dst) in enumerate(
            ((hidden, hid_v), (w_down, wd_v), (q_rope, qr_v), (q_latent, ql_v), (w_value, wv_v))
        )
    ]
    for load in loads:
        load.start()

    barrier = pltpu.get_barrier_semaphore()
    peers = [(seq, (tp + d) % TP) for d in range(1, TP)]
    peers += [device(x, y, (z + d) % 8) for d in range(1, 8)]
    peers += [sibling, device(x, 3 - y, z), device(x, (y + 2) % 4, z)]
    for peer in peers:
        pl.semaphore_signal(barrier, inc=1, device_id=peer, device_id_type=MESH)

    loads[0].wait()
    loads[1].wait()
    partial[...] = dot(hid_v[...], wd_v[...], NT)
    pl.semaphore_wait(barrier, len(peers))

    sent = []

    def copy(src, dst, send_sem, recv_sem, target):
        return pltpu.make_async_remote_copy(
            src_ref=src, dst_ref=dst, send_sem=send_sem, recv_sem=recv_sem, device_id=target, device_id_type=MESH
        )

    def start(cond, *args):
        one = copy(*args)
        maybe(cond, one.start)
        sent.append((cond, one))

    def rows_of(owner):
        return partial.at[pl.ds(pl.multiple_of(owner * SLICE, SLICE), SLICE), :]

    for d in range(1, TP):
        owner = (tp + d) % TP
        start(True, rows_of(owner), sums.at[d], rs_s.at[d], rs_r.at[d], (seq, owner))

    positions = (seq * TOK + lax.broadcasted_iota(jnp.int32, (TOK, 128), 0)).astype(jnp.float32)
    angles = positions * freq[...]
    lane = lax.broadcasted_iota(jnp.int32, (1, 128), 1)
    cos_t[...] = jnp.cos(angles)
    sin_t[...] = jnp.where(lane % ROPE < ROPE // 2, -jnp.sin(angles), jnp.sin(angles))
    loads[2].wait()
    raw = qr_v[...].astype(jnp.float32)
    wide_lane = lax.broadcasted_iota(jnp.int32, (1, HEADS * ROPE), 1)
    swapped = jnp.where(
        wide_lane % ROPE < ROPE // 2,
        pltpu.roll(raw, HEADS * ROPE - ROPE // 2, 1),
        pltpu.roll(raw, ROPE // 2, 1),
    )
    repeat = HEADS * ROPE // 128
    rotated = raw * jnp.concatenate([cos_t[...]] * repeat, 1) + swapped * jnp.concatenate([sin_t[...]] * repeat, 1)
    rotated = rotated.astype(jnp.bfloat16)
    loads[3].wait()
    for c in range(KV_RANK // 128):
        q_f32[c] = ql_v[:, c * 128:(c + 1) * 128].astype(jnp.float32)
    for h in range(HEADS):
        for c in range(KV_RANK // 128):
            queries[h * TOK:(h + 1) * TOK, c * 128:(c + 1) * 128] = q_f32[
                c, pl.ds(h, TOK, stride=HEADS), :
            ].astype(jnp.bfloat16)
        queries[h * TOK:(h + 1) * TOK, KV_RANK:] = rotated[:, h * ROPE:(h + 1) * ROPE]

    for d in range(1, TP):
        copy(rows_of(tp), sums.at[d], rs_s.at[d], rs_r.at[d], (seq, tp)).wait_recv()
    mine = pl.ds(pl.multiple_of(tp * SLICE, SLICE), SLICE)
    projection = partial[mine, :]
    for d in range(1, TP):
        projection = projection + sums[d]
    latent = projection[:, :KV_RANK]
    mean_square = jnp.mean(latent * latent, axis=-1, keepdims=True)
    latent = latent * lax.rsqrt(mean_square + EPSILON) * gain[...]
    rope = projection[:, KV_RANK:]
    rope_swapped = jnp.concatenate([rope[:, ROPE // 2:], rope[:, :ROPE // 2]], 1)
    rope = rope * cos_t[mine, :ROPE] + rope_swapped * sin_t[mine, :ROPE]

    def unit_at(lineage, a, b, part):
        first, second = PLACE[0, a, b, part], PLACE[1, a, b, part]
        place = first + (second - first) * lineage
        return keys.at[pl.ds(pl.multiple_of(place * HALF, HALF), HALF), :]

    def unit(a, b, part):
        return unit_at(core, a, b, part)

    own_place = [PLACE[0, ME, ME, part] + (PLACE[1, ME, ME, part] - PLACE[0, ME, ME, part]) * core for part in range(2)]

    def slot(z_):
        place = own_place[0] + (own_place[1] - own_place[0]) * (z_ // 4)
        return keys.at[pl.ds(pl.multiple_of(place * HALF + (z_ % 4) * SLICE, SLICE), SLICE), :]

    slot(z)[...] = jnp.concatenate([latent, rope], 1).astype(jnp.bfloat16)

    for d in (4, 3, 5, 2, 6, 1, 7):
        start(True, slot(z), slot(z), z_s.at[d], z_r.at[d], device(x, y, (z + d) % 8))
    for d in range(1, 8):
        there = slot((z - d) % 8)
        copy(there, there, z_s.at[d], z_r.at[d], sibling).wait_recv()

    early, late, even, odd = y_hi == 0, y_hi == 1, core == 0, core == 1

    def needed(lineage_even, a, b):
        if a in NEAR and b in NEAR:
            return True
        if b in NEAR:
            return late | lineage_even
        if a in NEAR:
            return late | jnp.logical_not(lineage_even)
        return late

    full = early | (z >= 4)

    def both(one, two):
        return two if one is True else one if two is True else one & two

    def kept(part, lineage_even, a, b):
        if part == 0 or not (a in NEAR or b in NEAR):
            return True
        if a in NEAR and b in NEAR:
            return full
        return full | (jnp.logical_not(lineage_even) if b in NEAR else lineage_even)

    def send_a(a):
        cond = True if a == MATE else even | early
        for part in range(2):
            start(
                both(cond, kept(part, even, a, ME)), unit(ME, ME, part), unit(a, ME, part),
                a_s.at[a, part], a_r.at[a, part], plane(near(a_me, a), b_me),
            )

    def send_b(a, b):
        if b == MATE:
            cond = True if a in NEAR else even | late
        else:
            cond = (even & early) | odd if a in NEAR else (even & early) | (odd & late)
        for part in range(2):
            start(
                both(cond, kept(part, even, a, b)), unit(a, ME, part), unit(a, b, part),
                b_s.at[b, a, part], b_r.at[b, a, part], plane(a_me, near(b_me, b)),
            )

    def to_sibling(a, b):
        for part in range(2):
            start(
                both(needed(even, a, b), kept(part, even, a, b)), unit(a, b, part), unit(a, b, part),
                c_s.at[b, a, part], c_r.at[b, a, part], sibling,
            )

    def arrived(lineage, lineage_even, a, b, recv_sem):
        for part in range(2):
            ref = unit_at(lineage, a, b, part)
            one = copy(ref, ref, c_s.at[0, 0, 0], recv_sem.at[part], sibling)
            maybe(both(needed(lineage_even, a, b), kept(part, lineage_even, a, b)), one.wait_recv)

    def got_a(a):
        arrived(core, even, a, ME, a_r.at[a])

    def got_b(a, b):
        arrived(core, even, a, b, b_r.at[b, a])

    def got_sibling(*labels):
        for a, b in labels:
            arrived(1 - core, odd, a, b, c_r.at[b, a])

    row = lax.broadcasted_iota(jnp.int32, (HALF, TOK), 0)
    token = lax.broadcasted_iota(jnp.int32, (HALF, TOK), 1)
    ahead = (row // SLICE) * (2 * TOK) + row % SLICE - token

    def bias(place):
        lineage, a, b, part = LABELS[place]
        x_label, y_label = (a, b) if lineage == 0 else (b, a)
        base = (lineage - core - 2 * z + 8 * part) * TOK + (near(x, x_label) * 2 + near(y, y_label) % 2) * SLICE
        return jnp.concatenate([jnp.where(ahead + base <= 0, 0.0, -1e30)] * (HEADS // 2), 1)

    def attend(half, begin, end, first=False):
        cut = slice(half * ROWS // 2, (half + 1) * ROWS // 2)
        rows = keys[begin * HALF:end * HALF, :]
        scores = dot(rows, queries[cut, :], NT)
        masked = [place for place in range(begin, end) if is_masked(*LABELS[place][:3])]
        if masked:
            low, high = (masked[0] - begin) * HALF, (masked[-1] + 1 - begin) * HALF
            blocks = [scores[low:high] + jnp.concatenate([bias(place) for place in masked], 0)]
            if low > 0:
                blocks.insert(0, scores[:low])
            if high < scores.shape[0]:
                blocks.append(scores[high:])
            scores = jnp.concatenate(blocks, 0)
        new_top = jnp.max(scores, 0, keepdims=True)
        if not first:
            new_top = jnp.maximum(top[0:1, cut], new_top)
        shift = new_top * EXP_SCALE
        weights = jnp.exp2(scores * EXP_SCALE - shift)
        added = jnp.sum(weights, 0, keepdims=True)
        mixed = dot(rows[:, :KV_RANK], weights.astype(jnp.bfloat16), TN)
        if first:
            total[0:1, cut] = added
            acc[:, cut] = mixed
        else:
            scale = jnp.exp2(top[0:1, cut] * EXP_SCALE - shift)
            total[0:1, cut] = total[0:1, cut] * scale + added
            acc[:, cut] = acc[:, cut] * scale + mixed
        top[0:1, cut] = new_top

    def chunk(half, stage):
        begin, masked_begin, masked_half, end = BOUNDS[stage]
        first = stage == 0
        if first:
            @pl.when(full)
            def _():
                attend(half, begin, end, first)
        else:
            @pl.when(early)
            def _():
                attend(half, masked_begin, end)

            @pl.when(late & full)
            def _():
                attend(half, begin, end)

        @pl.when(jnp.logical_not(full))
        def _():
            attend(half, begin, masked_half, first)

    away = (MATE, CROSS, FAR)
    for a in away:
        send_a(a)
    to_sibling(ME, ME)
    got_sibling((ME, ME))
    chunk(0, 0)
    for b in away:
        send_b(ME, b)
    chunk(1, 0)

    for a in away:
        got_a(a)
        for b in away:
            send_b(a, b)
        to_sibling(a, ME)
    got_sibling(*((a, ME) for a in away))
    for stage, a in enumerate((ME, *away), 1):
        chunk(0, stage)
        for b in away:
            got_b(a, b)
            to_sibling(a, b)
        chunk(1, stage)
        got_sibling(*((a, b) for b in away))
    chunk(0, 5)
    chunk(1, 5)

    loads[4].wait()
    mixed = (acc[...] * (1.0 / total[0:1, :])).astype(jnp.bfloat16)
    for h in range(HEADS):
        cut = slice(h * TOK, (h + 1) * TOK)
        out[:, h * V_DIM:(h + 1) * V_DIM] = dot(mixed[:, cut], wv_v[h], TN).astype(jnp.bfloat16)
    for cond, one in sent:
        maybe(cond, one.wait_send)


def shards(hidden, w_kv_down, kv_gain, q_latent, q_rope, w_value):
    half = ROPE // 2
    frequency = (10000.0 ** (-np.arange(half, dtype=np.float64) * 2.0 / ROPE)).astype(np.float32)
    freq = jnp.asarray(np.tile(frequency, 4)[None, :])
    hbm = pl.BlockSpec(memory_space=pl.ANY)
    vmem = pl.BlockSpec(memory_space=pltpu.VMEM)
    bf16, f32 = jnp.bfloat16, jnp.float32
    dma = pltpu.SemaphoreType.DMA
    width = hidden.shape[1]
    return pl.pallas_call(
        kernel,
        name="latent_attention",
        out_shape=jax.ShapeDtypeStruct((TOK, HEADS * V_DIM), bf16),
        in_specs=[hbm, hbm, vmem, hbm, hbm, hbm, vmem],
        out_specs=vmem,
        scratch_shapes=[
            pltpu.VMEM((TOK, width), bf16),
            pltpu.VMEM((WIDTH, width), bf16),
            pltpu.VMEM((ROWS, KV_RANK), bf16),
            pltpu.VMEM((TOK, HEADS * ROPE), bf16),
            pltpu.VMEM((HEADS, KV_RANK, V_DIM), bf16),
            pltpu.VMEM((TOK, WIDTH), f32),
            pltpu.VMEM((TP, SLICE, WIDTH), f32),
            pltpu.VMEM((64 * HALF, WIDTH), bf16),
            pltpu.VMEM((KV_RANK // 128, ROWS, 128), f32),
            pltpu.VMEM((ROWS, WIDTH), bf16),
            pltpu.VMEM((TOK, 128), f32),
            pltpu.VMEM((TOK, 128), f32),
            pltpu.VMEM((KV_RANK, ROWS), f32),
            pltpu.VMEM((8, ROWS), f32),
            pltpu.VMEM((8, ROWS), f32),
            dma((5,)),
            dma((8,)), dma((8,)),
            dma((8,)), dma((8,)),
            dma((4, 2)), dma((4, 2)),
            dma((4, 4, 2)), dma((4, 4, 2)),
            dma((4, 4, 2)), dma((4, 4, 2)),
        ],
        compiler_params=pltpu.CompilerParams(
            collective_id=0, has_side_effects=True, vmem_limit_bytes=60 * 2**20
        ),
    )(
        hidden,
        w_kv_down.T,
        kv_gain[None, :],
        q_latent.reshape(ROWS, KV_RANK),
        q_rope,
        w_value,
        freq,
    )


def solution(mesh):
    placed = (
        P("seq", "tp"),
        P("tp", None),
        P(),
        P("seq", "tp", None),
        P("seq", "tp"),
        P("tp", None, None),
    )
    return jax.shard_map(
        shards, mesh=mesh, in_specs=placed, out_specs=P("seq", "tp"), check_vma=False
    )
```

```python
import functools

import jax
import jax.numpy as jnp
import numpy as np
from jax import lax
from jax.experimental import pallas as pl
from jax.experimental.pallas import tpu as pltpu
from jax.sharding import PartitionSpec as P

MESH = pl.DeviceIdType.MESH
KV_RANK = 512
ROPE = 64
WIDTH = KV_RANK + ROPE
V_DIM = 128
TOK = 128
HEADS = 8
HALF = 64
ROWS = TOK * HEADS
TP = 8
SLICE = TOK // TP
EPSILON = 1e-06
LOG2E = 1.4426950408889634
EXP_SCALE = 192.0 ** (-0.5) * LOG2E
NT = (((1,), (1,)), ((), ()))
TN = (((0,), (0,)), ((), ()))


def dot(a, b, dims):
    return lax.dot_general(a, b, dims, preferred_element_type=jnp.float32)


def maybe(cond, act):
    if cond is True:
        act()
    else:
        pl.when(cond)(act)


ME, MATE, CROSS, FAR = range(4)
NEAR = (ME, MATE)


def near(i, label):
    sign = 1 - 2 * (i % 2)
    return (i + (0, sign, 4 - sign, 2)[label]) % 4


def is_masked(lineage, a, b):
    return (b, a)[lineage] in NEAR


def arrange():
    stages = (
        ((ME, ME),),
        ((MATE, ME), (CROSS, ME), (FAR, ME)),
        ((ME, MATE), (ME, CROSS), (ME, FAR)),
        ((MATE, MATE), (MATE, CROSS), (MATE, FAR)),
        ((CROSS, MATE), (CROSS, CROSS), (CROSS, FAR)),
        ((FAR, MATE), (FAR, CROSS), (FAR, FAR)),
    )
    labels, bounds = [], []
    for stage in stages:
        both = [(lineage, a, b) for lineage in range(2) for a, b in stage]
        free = [(*label, part) for label in both if not is_masked(*label) for part in range(2)]
        masked = [(*label, part) for part in range(2) for label in both if is_masked(*label)]
        start = len(labels)
        labels += free + masked
        bounds.append((start, start + len(free), start + len(free) + len(masked) // 2, len(labels)))
    return labels, bounds


LABELS, BOUNDS = arrange()
PLACE = {label: place for place, label in enumerate(LABELS)}


def kernel(
    hidden, w_down, gain, q_latent, q_rope, w_value, freq, out,
    hid_v, wd_v, ql_v, qr_v, wv_v, partial, sums, pieces, keys, q_f32, queries, cos_t, sin_t, acc, top, total,
    load_sem, rs_s, rs_r, z_s, z_r, a_s, a_r, b_s, b_r, c_s, c_r,
):
    seq = lax.axis_index("seq")
    tp = lax.axis_index("tp")
    core = seq % 2
    z = (seq // 2) % 8
    y_hi = seq // 16
    x = tp // 2
    y_lo = tp % 2
    y = y_hi * 2 + y_lo

    def device(x_, y_, z_):
        return (((y_ // 2) * 8 + z_) * 2 + core, x_ * 2 + y_ % 2)

    a_me = x * (1 - core) + y * core
    b_me = y * (1 - core) + x * core

    def plane(a_, b_):
        return device(a_ * (1 - core) + b_ * core, b_ * (1 - core) + a_ * core, z)

    sibling = (seq + 1 - 2 * core, tp)

    loads = [
        pltpu.make_async_copy(src, dst, load_sem.at[i])
        for i, (src, dst) in enumerate(
            ((hidden, hid_v), (w_down, wd_v), (q_rope, qr_v), (q_latent, ql_v), (w_value, wv_v))
        )
    ]
    for load in loads:
        load.start()

    barrier = pltpu.get_barrier_semaphore()
    peers = [(seq, (tp + d) % TP) for d in range(1, TP)]
    peers += [device(x, y, (z + d) % 8) for d in range(1, 8)]
    peers += [sibling, device(x, 3 - y, z), device(x, (y + 2) % 4, z)]
    for peer in peers:
        pl.semaphore_signal(barrier, inc=1, device_id=peer, device_id_type=MESH)

    loads[0].wait()
    loads[1].wait()
    partial[...] = dot(hid_v[...], wd_v[...], NT)
    pl.semaphore_wait(barrier, len(peers))

    sent = []

    def copy(src, dst, send_sem, recv_sem, target):
        return pltpu.make_async_remote_copy(
            src_ref=src, dst_ref=dst, send_sem=send_sem, recv_sem=recv_sem, device_id=target, device_id_type=MESH
        )

    def start(cond, *args):
        one = copy(*args)
        maybe(cond, one.start)
        sent.append((cond, one))

    def rows_of(owner):
        return partial.at[pl.ds(pl.multiple_of(owner * SLICE, SLICE), SLICE), :]

    for d in range(1, TP):
        owner = (tp + d) % TP
        start(True, rows_of(owner), sums.at[d], rs_s.at[d], rs_r.at[d], (seq, owner))

    positions = (seq * TOK + lax.broadcasted_iota(jnp.int32, (TOK, 128), 0)).astype(jnp.float32)
    angles = positions * freq[...]
    lane = lax.broadcasted_iota(jnp.int32, (1, 128), 1)
    cos_t[...] = jnp.cos(angles)
    sin_t[...] = jnp.where(lane % ROPE < ROPE // 2, -jnp.sin(angles), jnp.sin(angles))
    loads[2].wait()
    raw = qr_v[...].astype(jnp.float32)
    wide_lane = lax.broadcasted_iota(jnp.int32, (1, HEADS * ROPE), 1)
    swapped = jnp.where(
        wide_lane % ROPE < ROPE // 2,
        pltpu.roll(raw, HEADS * ROPE - ROPE // 2, 1),
        pltpu.roll(raw, ROPE // 2, 1),
    )
    repeat = HEADS * ROPE // 128
    rotated = raw * jnp.concatenate([cos_t[...]] * repeat, 1) + swapped * jnp.concatenate([sin_t[...]] * repeat, 1)
    rotated = rotated.astype(jnp.bfloat16)
    loads[3].wait()
    for c in range(KV_RANK // 128):
        q_f32[c] = ql_v[:, c * 128:(c + 1) * 128].astype(jnp.float32)
    for h in range(HEADS):
        for c in range(KV_RANK // 128):
            queries[h * TOK:(h + 1) * TOK, c * 128:(c + 1) * 128] = q_f32[
                c, pl.ds(h, TOK, stride=HEADS), :
            ].astype(jnp.bfloat16)
        mine = rotated[:, h * ROPE:(h + 1) * ROPE]
        queries[h * TOK:(h + 1) * TOK, KV_RANK:] = jnp.concatenate([mine, mine], 1)

    for d in range(1, TP):
        copy(rows_of(tp), sums.at[d], rs_s.at[d], rs_r.at[d], (seq, tp)).wait_recv()
    mine = pl.ds(pl.multiple_of(tp * SLICE, SLICE), SLICE)
    projection = partial[mine, :]
    for d in range(1, TP):
        projection = projection + sums[d]
    latent = projection[:, :KV_RANK]
    mean_square = jnp.mean(latent * latent, axis=-1, keepdims=True)
    latent = latent * lax.rsqrt(mean_square + EPSILON) * gain[...]
    rope = projection[:, KV_RANK:]
    rope_swapped = jnp.concatenate([rope[:, ROPE // 2:], rope[:, :ROPE // 2]], 1)
    rope = rope * cos_t[mine, :ROPE] + rope_swapped * sin_t[mine, :ROPE]

    def unit_at(lineage, a, b, part):
        first, second = PLACE[0, a, b, part], PLACE[1, a, b, part]
        place = first + (second - first) * lineage
        return keys.at[place]

    def unit(a, b, part):
        return unit_at(core, a, b, part)

    own_place = [PLACE[0, ME, ME, part] + (PLACE[1, ME, ME, part] - PLACE[0, ME, ME, part]) * core for part in range(2)]

    def slot(z_):
        return pieces.at[z_]

    slot(z)[...] = jnp.concatenate([latent, rope], 1).astype(jnp.bfloat16)

    for d in (4, 3, 5, 2, 6, 1, 7):
        start(True, slot(z), slot(z), z_s.at[d], z_r.at[d], device(x, y, (z + d) % 8))
    for d in range(1, 8):
        there = slot((z - d) % 8)
        copy(there, there, z_s.at[d], z_r.at[d], sibling).wait_recv()
    for part in range(2):
        four = [pieces[part * 4 + i] for i in range(4)]
        for i in range(4):
            for c in range(KV_RANK // 128):
                keys[own_place[part], c * HALF + i * SLICE:c * HALF + (i + 1) * SLICE, :] = four[i][:, c * 128:(c + 1) * 128]
        for i in range(2):
            at = KV_RANK // 128 * HALF + i * SLICE
            keys[own_place[part], at:at + SLICE, :] = jnp.concatenate([four[i][:, KV_RANK:], four[i + 2][:, KV_RANK:]], 1)

    early, late, even, odd = y_hi == 0, y_hi == 1, core == 0, core == 1

    def needed(lineage_even, a, b):
        if a in NEAR and b in NEAR:
            return True
        if b in NEAR:
            return late | lineage_even
        if a in NEAR:
            return late | jnp.logical_not(lineage_even)
        return late

    full = early | (z >= 4)

    def both(one, two):
        return two if one is True else one if two is True else one & two

    def kept(part, lineage_even, a, b):
        if part == 0 or not (a in NEAR or b in NEAR):
            return True
        if a in NEAR and b in NEAR:
            return full
        return full | (jnp.logical_not(lineage_even) if b in NEAR else lineage_even)

    def send_a(a):
        cond = True if a == MATE else even | early
        for part in range(2):
            start(
                both(cond, kept(part, even, a, ME)), unit(ME, ME, part), unit(a, ME, part),
                a_s.at[a, part], a_r.at[a, part], plane(near(a_me, a), b_me),
            )

    def send_b(a, b):
        if b == MATE:
            cond = True if a in NEAR else even | late
        else:
            cond = (even & early) | odd if a in NEAR else (even & early) | (odd & late)
        for part in range(2):
            start(
                both(cond, kept(part, even, a, b)), unit(a, ME, part), unit(a, b, part),
                b_s.at[b, a, part], b_r.at[b, a, part], plane(a_me, near(b_me, b)),
            )

    def to_sibling(a, b):
        for part in range(2):
            start(
                both(needed(even, a, b), kept(part, even, a, b)), unit(a, b, part), unit(a, b, part),
                c_s.at[b, a, part], c_r.at[b, a, part], sibling,
            )

    def arrived(lineage, lineage_even, a, b, recv_sem):
        for part in range(2):
            ref = unit_at(lineage, a, b, part)
            one = copy(ref, ref, c_s.at[0, 0, 0], recv_sem.at[part], sibling)
            maybe(both(needed(lineage_even, a, b), kept(part, lineage_even, a, b)), one.wait_recv)

    def got_a(a):
        arrived(core, even, a, ME, a_r.at[a])

    def got_b(a, b):
        arrived(core, even, a, b, b_r.at[b, a])

    def got_sibling(*labels):
        for a, b in labels:
            arrived(1 - core, odd, a, b, c_r.at[b, a])

    row = lax.broadcasted_iota(jnp.int32, (HALF, TOK), 0)
    token = lax.broadcasted_iota(jnp.int32, (HALF, TOK), 1)
    ahead = (row // SLICE) * (2 * TOK) + row % SLICE - token

    def bias(place):
        lineage, a, b, part = LABELS[place]
        x_label, y_label = (a, b) if lineage == 0 else (b, a)
        base = (lineage - core - 2 * z + 8 * part) * TOK + (near(x, x_label) * 2 + near(y, y_label) % 2) * SLICE
        return jnp.concatenate([jnp.where(ahead + base <= 0, 0.0, -1e30)] * (HEADS // 2), 1)

    sides = [(lane < ROPE).astype(jnp.bfloat16), (lane >= ROPE).astype(jnp.bfloat16)]

    def attend(half, begin, end, first=False):
        cut = slice(half * ROWS // 2, (half + 1) * ROWS // 2)
        blocks = range(begin, end)
        rows = jnp.concatenate(
            [
                jnp.concatenate([keys[place, c * HALF:(c + 1) * HALF, :] for place in blocks], 0)
                for c in range(KV_RANK // 128)
            ],
            1,
        )
        pairs = [keys[place, KV_RANK // 128 * HALF:, :] for place in blocks]
        ropes = jnp.concatenate([side * pair for pair in pairs for side in sides], 0)
        scores = dot(jnp.concatenate([rows, ropes], 1), queries[cut, :], NT)
        masked = [place for place in range(begin, end) if is_masked(*LABELS[place][:3])]
        if masked:
            low, high = (masked[0] - begin) * HALF, (masked[-1] + 1 - begin) * HALF
            split = [scores[low:high] + jnp.concatenate([bias(place) for place in masked], 0)]
            if low > 0:
                split.insert(0, scores[:low])
            if high < scores.shape[0]:
                split.append(scores[high:])
            scores = jnp.concatenate(split, 0)
        new_top = jnp.max(scores, 0, keepdims=True)
        if not first:
            new_top = jnp.maximum(top[0:1, cut], new_top)
        shift = new_top * EXP_SCALE
        weights = jnp.exp2(scores * EXP_SCALE - shift)
        added = jnp.sum(weights, 0, keepdims=True)
        mixed = dot(rows, weights.astype(jnp.bfloat16), TN)
        if first:
            total[0:1, cut] = added
            acc[:, cut] = mixed
        else:
            scale = jnp.exp2(top[0:1, cut] * EXP_SCALE - shift)
            total[0:1, cut] = total[0:1, cut] * scale + added
            acc[:, cut] = acc[:, cut] * scale + mixed
        top[0:1, cut] = new_top

    def chunk(half, stage):
        begin, masked_begin, masked_half, end = BOUNDS[stage]
        first = stage == 0
        if first:
            pl.when(full)(lambda: attend(half, begin, end, first))
        else:
            pl.when(early)(lambda: attend(half, masked_begin, end))
            pl.when(late & full)(lambda: attend(half, begin, end))
        pl.when(jnp.logical_not(full))(lambda: attend(half, begin, masked_half, first))

    away = (MATE, CROSS, FAR)
    for a in away:
        send_a(a)
    to_sibling(ME, ME)
    got_sibling((ME, ME))
    chunk(0, 0)
    for b in away:
        send_b(ME, b)
    chunk(1, 0)

    for a in away:
        got_a(a)
        for b in away:
            send_b(a, b)
        to_sibling(a, ME)
    got_sibling(*((a, ME) for a in away))
    for stage, a in enumerate((ME, *away), 1):
        chunk(0, stage)
        for b in away:
            got_b(a, b)
            to_sibling(a, b)
        chunk(1, stage)
        got_sibling(*((a, b) for b in away))
    chunk(0, 5)
    chunk(1, 5)

    loads[4].wait()
    mixed = (acc[...] * (1.0 / total[0:1, :])).astype(jnp.bfloat16)
    for h in range(HEADS):
        cut = slice(h * TOK, (h + 1) * TOK)
        out[:, h * V_DIM:(h + 1) * V_DIM] = dot(mixed[:, cut], wv_v[h], TN).astype(jnp.bfloat16)
    for cond, one in sent:
        maybe(cond, one.wait_send)


def shards(hidden, w_kv_down, kv_gain, q_latent, q_rope, w_value):
    half = ROPE // 2
    frequency = (10000.0 ** (-np.arange(half, dtype=np.float64) * 2.0 / ROPE)).astype(np.float32)
    freq = jnp.asarray(np.tile(frequency, 4)[None, :])
    hbm = pl.BlockSpec(memory_space=pl.ANY)
    vmem = pl.BlockSpec(memory_space=pltpu.VMEM)
    bf16, f32 = jnp.bfloat16, jnp.float32
    dma = pltpu.SemaphoreType.DMA
    width = hidden.shape[1]
    return pl.pallas_call(
        kernel,
        name="latent_attention",
        out_shape=jax.ShapeDtypeStruct((TOK, HEADS * V_DIM), bf16),
        in_specs=[hbm, hbm, vmem, hbm, hbm, hbm, vmem],
        out_specs=vmem,
        scratch_shapes=[
            pltpu.VMEM((TOK, width), bf16),
            pltpu.VMEM((WIDTH, width), bf16),
            pltpu.VMEM((ROWS, KV_RANK), bf16),
            pltpu.VMEM((TOK, HEADS * ROPE), bf16),
            pltpu.VMEM((HEADS, KV_RANK, V_DIM), bf16),
            pltpu.VMEM((TOK, WIDTH), f32),
            pltpu.VMEM((TP, SLICE, WIDTH), f32),
            pltpu.VMEM((8, SLICE, WIDTH), bf16),
            pltpu.VMEM((64, HALF // 2 * 9, 128), bf16),
            pltpu.VMEM((KV_RANK // 128, ROWS, 128), f32),
            pltpu.VMEM((ROWS, WIDTH + ROPE), bf16),
            pltpu.VMEM((TOK, 128), f32),
            pltpu.VMEM((TOK, 128), f32),
            pltpu.VMEM((KV_RANK, ROWS), f32),
            pltpu.VMEM((8, ROWS), f32),
            pltpu.VMEM((8, ROWS), f32),
            dma((5,)),
            dma((8,)), dma((8,)),
            dma((8,)), dma((8,)),
            dma((4, 2)), dma((4, 2)),
            dma((4, 4, 2)), dma((4, 4, 2)),
            dma((4, 4, 2)), dma((4, 4, 2)),
        ],
        compiler_params=pltpu.CompilerParams(
            collective_id=0, has_side_effects=True, vmem_limit_bytes=60 * 2**20
        ),
    )(
        hidden,
        w_kv_down.T,
        kv_gain[None, :],
        q_latent.reshape(ROWS, KV_RANK),
        q_rope,
        w_value,
        freq,
    )


def solution(mesh):
    placed = (
        P("seq", "tp"),
        P("tp", None),
        P(),
        P("seq", "tp", None),
        P("seq", "tp"),
        P("tp", None, None),
    )
    return jax.shard_map(
        shards, mesh=mesh, in_specs=placed, out_specs=P("seq", "tp"), check_vma=False
    )
```

```python
import functools

import jax
import jax.numpy as jnp
import numpy as np
from jax import lax
from jax.experimental import pallas as pl
from jax.experimental.pallas import tpu as pltpu
from jax.sharding import PartitionSpec as P

MESH = pl.DeviceIdType.MESH
KV_RANK = 512
ROPE = 64
WIDTH = KV_RANK + ROPE
V_DIM = 128
TOK = 128
HEADS = 8
HALF = 64
ROWS = TOK * HEADS
TP = 8
SLICE = TOK // TP
EPSILON = 1e-06
LOG2E = 1.4426950408889634
EXP_SCALE = 192.0 ** (-0.5) * LOG2E
NT = (((1,), (1,)), ((), ()))
TN = (((0,), (0,)), ((), ()))


def dot(a, b, dims):
    return lax.dot_general(a, b, dims, preferred_element_type=jnp.float32)


def maybe(cond, act):
    if cond is True:
        act()
    else:
        pl.when(cond)(act)


ME, MATE, CROSS, FAR = range(4)
NEAR = (ME, MATE)


def near(i, label):
    sign = 1 - 2 * (i % 2)
    return (i + (0, sign, 4 - sign, 2)[label]) % 4


def is_masked(lineage, a, b):
    return (b, a)[lineage] in NEAR


def arrange():
    stages = (
        ((ME, ME),),
        ((MATE, ME), (CROSS, ME), (FAR, ME)),
        ((ME, MATE), (ME, CROSS), (ME, FAR)),
        ((MATE, MATE), (MATE, CROSS), (MATE, FAR)),
        ((CROSS, MATE), (CROSS, CROSS), (CROSS, FAR)),
        ((FAR, MATE), (FAR, CROSS), (FAR, FAR)),
    )
    labels, bounds = [], []
    for stage in stages:
        both = [(lineage, a, b) for lineage in range(2) for a, b in stage]
        free = [(*label, part) for label in both[::-1] if not is_masked(*label) for part in range(2)]
        masked = [(*label, part) for part in range(2) for label in both if is_masked(*label)]
        start = len(labels)
        labels += free + masked
        bounds.append((start, start + len(free), start + len(free) + len(masked) // 2, len(labels)))
    return labels, bounds


LABELS, BOUNDS = arrange()
PLACE = {label: place for place, label in enumerate(LABELS)}


def kernel(
    hidden, w_down, gain, q_latent, q_rope, w_value, freq, out,
    hid_v, wd_v, ql_v, qr_v, wv_v, partial, sums, pieces, keys, q_f32, queries, cos_t, sin_t, acc, top, total,
    load_sem, rs_s, rs_r, z_s, z_r, a_s, a_r, b_s, b_r, c_s, c_r,
):
    seq = lax.axis_index("seq")
    tp = lax.axis_index("tp")
    core = seq % 2
    z = (seq // 2) % 8
    y_hi = seq // 16
    x = tp // 2
    y_lo = tp % 2
    y = y_hi * 2 + y_lo

    def device(x_, y_, z_):
        return (((y_ // 2) * 8 + z_) * 2 + core, x_ * 2 + y_ % 2)

    a_me = x * (1 - core) + y * core
    b_me = y * (1 - core) + x * core

    def plane(a_, b_):
        return device(a_ * (1 - core) + b_ * core, b_ * (1 - core) + a_ * core, z)

    sibling = (seq + 1 - 2 * core, tp)

    loads = [
        pltpu.make_async_copy(src, dst, load_sem.at[i])
        for i, (src, dst) in enumerate(
            ((hidden, hid_v), (w_down, wd_v), (q_rope, qr_v), (q_latent, ql_v), (w_value, wv_v))
        )
    ]
    for load in loads:
        load.start()

    barrier = pltpu.get_barrier_semaphore()
    peers = [(seq, (tp + d) % TP) for d in range(1, TP)]
    peers += [device(x, y, (z + d) % 8) for d in range(1, 8)]
    peers += [sibling, device(x, 3 - y, z), device(x, (y + 2) % 4, z)]
    for peer in peers:
        pl.semaphore_signal(barrier, inc=1, device_id=peer, device_id_type=MESH)

    loads[0].wait()
    loads[1].wait()
    partial[...] = dot(hid_v[...], wd_v[...], NT)
    pl.semaphore_wait(barrier, len(peers))

    sent = []

    def copy(src, dst, send_sem, recv_sem, target):
        return pltpu.make_async_remote_copy(
            src_ref=src, dst_ref=dst, send_sem=send_sem, recv_sem=recv_sem, device_id=target, device_id_type=MESH
        )

    def start(cond, *args):
        one = copy(*args)
        maybe(cond, one.start)
        sent.append((cond, one))

    def rows_of(owner):
        return partial.at[pl.ds(pl.multiple_of(owner * SLICE, SLICE), SLICE), :]

    for d in range(1, TP):
        owner = (tp + d) % TP
        start(True, rows_of(owner), sums.at[d], rs_s.at[d], rs_r.at[d], (seq, owner))

    positions = (seq * TOK + lax.broadcasted_iota(jnp.int32, (TOK, 128), 0)).astype(jnp.float32)
    angles = positions * freq[...]
    lane = lax.broadcasted_iota(jnp.int32, (1, 128), 1)
    cos_t[...] = jnp.cos(angles)
    sin_t[...] = jnp.where(lane % ROPE < ROPE // 2, -jnp.sin(angles), jnp.sin(angles))
    loads[2].wait()
    raw = qr_v[...].astype(jnp.float32)
    wide_lane = lax.broadcasted_iota(jnp.int32, (1, HEADS * ROPE), 1)
    swapped = jnp.where(
        wide_lane % ROPE < ROPE // 2,
        pltpu.roll(raw, HEADS * ROPE - ROPE // 2, 1),
        pltpu.roll(raw, ROPE // 2, 1),
    )
    repeat = HEADS * ROPE // 128
    rotated = raw * jnp.concatenate([cos_t[...]] * repeat, 1) + swapped * jnp.concatenate([sin_t[...]] * repeat, 1)
    rotated = rotated.astype(jnp.bfloat16)
    loads[3].wait()
    for c in range(KV_RANK // 128):
        q_f32[c] = ql_v[:, c * 128:(c + 1) * 128].astype(jnp.float32)
    for h in range(HEADS):
        for c in range(KV_RANK // 128):
            queries[h * TOK:(h + 1) * TOK, c * 128:(c + 1) * 128] = q_f32[
                c, pl.ds(h, TOK, stride=HEADS), :
            ].astype(jnp.bfloat16)
        mine = rotated[:, h * ROPE:(h + 1) * ROPE]
        queries[h * TOK:(h + 1) * TOK, KV_RANK:] = jnp.concatenate([mine, mine], 1)

    for d in range(1, TP):
        copy(rows_of(tp), sums.at[d], rs_s.at[d], rs_r.at[d], (seq, tp)).wait_recv()
    mine = pl.ds(pl.multiple_of(tp * SLICE, SLICE), SLICE)
    projection = partial[mine, :]
    for d in range(1, TP):
        projection = projection + sums[d]
    latent = projection[:, :KV_RANK]
    mean_square = jnp.mean(latent * latent, axis=-1, keepdims=True)
    latent = latent * lax.rsqrt(mean_square + EPSILON) * gain[...]
    rope = projection[:, KV_RANK:]
    rope_swapped = jnp.concatenate([rope[:, ROPE // 2:], rope[:, :ROPE // 2]], 1)
    rope = rope * cos_t[mine, :ROPE] + rope_swapped * sin_t[mine, :ROPE]

    def unit_at(lineage, a, b, part):
        first, second = PLACE[0, a, b, part], PLACE[1, a, b, part]
        place = first + (second - first) * lineage
        return keys.at[place]

    def unit(a, b, part):
        return unit_at(core, a, b, part)

    own_place = [PLACE[0, ME, ME, part] + (PLACE[1, ME, ME, part] - PLACE[0, ME, ME, part]) * core for part in range(2)]

    def slot(z_):
        return pieces.at[z_]

    slot(z)[...] = jnp.concatenate([latent, rope], 1).astype(jnp.bfloat16)

    for d in (4, 3, 5, 2, 6, 1, 7):
        start(True, slot(z), slot(z), z_s.at[d], z_r.at[d], device(x, y, (z + d) % 8))
    for d in range(1, 8):
        there = slot((z - d) % 8)
        copy(there, there, z_s.at[d], z_r.at[d], sibling).wait_recv()
    for part in range(2):
        four = [pieces[part * 4 + i] for i in range(4)]
        for i in range(4):
            for c in range(KV_RANK // 128):
                keys[own_place[part], c * HALF + i * SLICE:c * HALF + (i + 1) * SLICE, :] = four[i][:, c * 128:(c + 1) * 128]
        for i in range(2):
            at = KV_RANK // 128 * HALF + i * SLICE
            keys[own_place[part], at:at + SLICE, :] = jnp.concatenate([four[i][:, KV_RANK:], four[i + 2][:, KV_RANK:]], 1)

    early, late, even, odd = y_hi == 0, y_hi == 1, core == 0, core == 1

    def needed(lineage_even, a, b):
        if a in NEAR and b in NEAR:
            return True
        if b in NEAR:
            return late | lineage_even
        if a in NEAR:
            return late | jnp.logical_not(lineage_even)
        return late

    full = early | (z >= 4)

    def both(one, two):
        return two if one is True else one if two is True else one & two

    def kept(part, lineage_even, a, b):
        if part == 0 or not (a in NEAR or b in NEAR):
            return True
        if a in NEAR and b in NEAR:
            return full
        return full | (jnp.logical_not(lineage_even) if b in NEAR else lineage_even)

    def send_a(a):
        cond = True if a == MATE else even | early
        for part in range(2):
            start(
                both(cond, kept(part, even, a, ME)), unit(ME, ME, part), unit(a, ME, part),
                a_s.at[a, part], a_r.at[a, part], plane(near(a_me, a), b_me),
            )

    def send_b(a, b):
        if b == MATE:
            cond = True if a in NEAR else even | late
        else:
            cond = (even & early) | odd if a in NEAR else (even & early) | (odd & late)
        for part in range(2):
            start(
                both(cond, kept(part, even, a, b)), unit(a, ME, part), unit(a, b, part),
                b_s.at[b, a, part], b_r.at[b, a, part], plane(a_me, near(b_me, b)),
            )

    def to_sibling(a, b):
        for part in range(2):
            start(
                both(needed(even, a, b), kept(part, even, a, b)), unit(a, b, part), unit(a, b, part),
                c_s.at[b, a, part], c_r.at[b, a, part], sibling,
            )

    def arrived(lineage, lineage_even, a, b, recv_sem):
        for part in range(2):
            ref = unit_at(lineage, a, b, part)
            one = copy(ref, ref, c_s.at[0, 0, 0], recv_sem.at[part], sibling)
            maybe(both(needed(lineage_even, a, b), kept(part, lineage_even, a, b)), one.wait_recv)

    def got_a(a):
        arrived(core, even, a, ME, a_r.at[a])

    def got_b(a, b):
        arrived(core, even, a, b, b_r.at[b, a])

    def got_sibling(*labels):
        for a, b in labels:
            arrived(1 - core, odd, a, b, c_r.at[b, a])

    row = lax.broadcasted_iota(jnp.int32, (HALF, TOK), 0)
    token = lax.broadcasted_iota(jnp.int32, (HALF, TOK), 1)
    ahead = (row // SLICE) * (2 * TOK) + row % SLICE - token

    def bias(place):
        lineage, a, b, part = LABELS[place]
        x_label, y_label = (a, b) if lineage == 0 else (b, a)
        base = (lineage - core - 2 * z + 8 * part) * TOK + (near(x, x_label) * 2 + near(y, y_label) % 2) * SLICE
        return jnp.concatenate([jnp.where(ahead + base <= 0, 0.0, -1e30)] * (HEADS // 2), 1)

    sides = [(lane < ROPE).astype(jnp.bfloat16), (lane >= ROPE).astype(jnp.bfloat16)]

    def attend(halves, begin, end, first=False):
        blocks = range(begin, end)
        rows = jnp.concatenate(
            [
                jnp.concatenate([keys[place, c * HALF:(c + 1) * HALF, :] for place in blocks], 0)
                for c in range(KV_RANK // 128)
            ],
            1,
        )
        pairs = [keys[place, KV_RANK // 128 * HALF:, :] for place in blocks]
        ropes = jnp.concatenate([side * pair for pair in pairs for side in sides], 0)
        wide_rows = jnp.concatenate([rows, ropes], 1)
        masked = [place for place in blocks if is_masked(*LABELS[place][:3])]
        low = (masked[0] - begin) * HALF if masked else 0
        high = (masked[-1] + 1 - begin) * HALF if masked else 0
        mask = jnp.concatenate([bias(place) for place in masked], 0) if masked else None
        cuts = [slice(half * ROWS // 2, (half + 1) * ROWS // 2) for half in halves]

        def scores_of(cut):
            scores = dot(wide_rows, queries[cut, :], NT)
            if masked:
                split = [scores[low:high] + mask]
                if low > 0:
                    split.insert(0, scores[:low])
                if high < scores.shape[0]:
                    split.append(scores[high:])
                scores = jnp.concatenate(split, 0)
            return scores

        def weights_of(cut, scores):
            new_top = jnp.max(scores, 0, keepdims=True)
            scale = None
            if not first:
                new_top = jnp.maximum(top[0:1, cut], new_top)
            shift = new_top * EXP_SCALE
            weights = jnp.exp2(scores * EXP_SCALE - shift)
            added = jnp.sum(weights, 0, keepdims=True)
            if first:
                total[0:1, cut] = added
            else:
                scale = jnp.exp2(top[0:1, cut] * EXP_SCALE - shift)
                total[0:1, cut] = total[0:1, cut] * scale + added
            top[0:1, cut] = new_top
            return weights.astype(jnp.bfloat16), scale

        all_scores = [scores_of(cut) for cut in cuts]
        all_weights = [weights_of(cut, scores) for cut, scores in zip(cuts, all_scores)]
        for cut, (weights, scale) in zip(cuts, all_weights):
            mixed = dot(rows, weights, TN)
            acc[:, cut] = mixed if first else acc[:, cut] * scale + mixed

    def chunk(stage, halves=(0, 1)):
        begin, masked_begin, masked_half, end = BOUNDS[stage]
        first = stage == 0
        if first:
            pl.when(full)(lambda: attend(halves, begin, end, first))
        else:
            pl.when(early)(lambda: attend(halves, masked_begin, end))
            pl.when(late & full)(lambda: attend(halves, begin, end))
        pl.when(jnp.logical_not(full))(lambda: attend(halves, begin, masked_half, first))

    away = (MATE, CROSS, FAR)

    def landed(a):
        for b in away:
            got_b(a, b)
            to_sibling(a, b)

    def shared(a):
        got_sibling(*((a, b) for b in away))

    order = (MATE, CROSS, FAR)
    for a in order:
        send_a(a)
    to_sibling(ME, ME)
    got_sibling((ME, ME))
    for b in order:
        send_b(ME, b)
    chunk(0)
    for a in away:
        got_a(a)
        for b in order:
            send_b(a, b)
        to_sibling(a, ME)
    got_sibling(*((a, ME) for a in away))
    landed(ME)
    chunk(1)
    shared(ME)
    landed(MATE)
    chunk(2)
    shared(MATE)
    chunk(3, (0,))
    landed(CROSS)
    chunk(3, (1,))
    shared(CROSS)
    chunk(4)
    landed(FAR)
    begin, masked_begin, masked_half, last = BOUNDS[5]
    middle = begin + 6

    def even_lineage():
        pl.when(early)(lambda: attend((0, 1), masked_begin, last))
        pl.when(late & full)(lambda: attend((0, 1), middle, last))
        pl.when(jnp.logical_not(full))(lambda: attend((0, 1), middle, masked_half))

    def odd_lineage():
        pl.when(late)(lambda: attend((0, 1), begin, middle))

    pl.when(even)(even_lineage)
    pl.when(odd)(odd_lineage)
    shared(FAR)
    pl.when(even)(odd_lineage)
    pl.when(odd)(even_lineage)


    loads[4].wait()
    mixed = (acc[...] * (1.0 / total[0:1, :])).astype(jnp.bfloat16)
    for h in range(HEADS):
        cut = slice(h * TOK, (h + 1) * TOK)
        out[:, h * V_DIM:(h + 1) * V_DIM] = dot(mixed[:, cut], wv_v[h], TN).astype(jnp.bfloat16)
    for cond, one in sent:
        maybe(cond, one.wait_send)


def shards(hidden, w_kv_down, kv_gain, q_latent, q_rope, w_value):
    half = ROPE // 2
    frequency = (10000.0 ** (-np.arange(half, dtype=np.float64) * 2.0 / ROPE)).astype(np.float32)
    freq = jnp.asarray(np.tile(frequency, 4)[None, :])
    hbm = pl.BlockSpec(memory_space=pl.ANY)
    vmem = pl.BlockSpec(memory_space=pltpu.VMEM)
    bf16, f32 = jnp.bfloat16, jnp.float32
    dma = pltpu.SemaphoreType.DMA
    width = hidden.shape[1]
    return pl.pallas_call(
        kernel,
        name="latent_attention",
        out_shape=jax.ShapeDtypeStruct((TOK, HEADS * V_DIM), bf16),
        in_specs=[hbm, hbm, vmem, hbm, hbm, hbm, vmem],
        out_specs=vmem,
        scratch_shapes=[
            pltpu.VMEM((TOK, width), bf16),
            pltpu.VMEM((WIDTH, width), bf16),
            pltpu.VMEM((ROWS, KV_RANK), bf16),
            pltpu.VMEM((TOK, HEADS * ROPE), bf16),
            pltpu.VMEM((HEADS, KV_RANK, V_DIM), bf16),
            pltpu.VMEM((TOK, WIDTH), f32),
            pltpu.VMEM((TP, SLICE, WIDTH), f32),
            pltpu.VMEM((8, SLICE, WIDTH), bf16),
            pltpu.VMEM((64, HALF // 2 * 9, 128), bf16),
            pltpu.VMEM((KV_RANK // 128, ROWS, 128), f32),
            pltpu.VMEM((ROWS, WIDTH + ROPE), bf16),
            pltpu.VMEM((TOK, 128), f32),
            pltpu.VMEM((TOK, 128), f32),
            pltpu.VMEM((KV_RANK, ROWS), f32),
            pltpu.VMEM((8, ROWS), f32),
            pltpu.VMEM((8, ROWS), f32),
            dma((5,)),
            dma((8,)), dma((8,)),
            dma((8,)), dma((8,)),
            dma((4, 2)), dma((4, 2)),
            dma((4, 4, 2)), dma((4, 4, 2)),
            dma((4, 4, 2)), dma((4, 4, 2)),
        ],
        compiler_params=pltpu.CompilerParams(
            collective_id=0, has_side_effects=True, vmem_limit_bytes=60 * 2**20
        ),
    )(
        hidden,
        w_kv_down.T,
        kv_gain[None, :],
        q_latent.reshape(ROWS, KV_RANK),
        q_rope,
        w_value,
        freq,
    )


def solution(mesh):
    placed = (
        P("seq", "tp"),
        P("tp", None),
        P(),
        P("seq", "tp", None),
        P("seq", "tp"),
        P("tp", None, None),
    )
    return jax.shard_map(
        shards, mesh=mesh, in_specs=placed, out_specs=P("seq", "tp"), check_vma=False
    )
```

```python
import functools

import jax
import jax.numpy as jnp
import numpy as np
from jax import lax
from jax.experimental import pallas as pl
from jax.experimental.pallas import tpu as pltpu
from jax.sharding import PartitionSpec as P

MESH = pl.DeviceIdType.MESH
KV_RANK = 512
ROPE = 64
WIDTH = KV_RANK + ROPE
V_DIM = 128
TOK = 128
HEADS = 8
HALF = 64
ROWS = TOK * HEADS
TP = 8
SLICE = TOK // TP
EPSILON = 1e-06
LOG2E = 1.4426950408889634
EXP_SCALE = 192.0 ** (-0.5) * LOG2E
NT = (((1,), (1,)), ((), ()))
TN = (((0,), (0,)), ((), ()))


def dot(a, b, dims):
    return lax.dot_general(a, b, dims, preferred_element_type=jnp.float32)


def maybe(cond, act):
    if cond is True:
        act()
    else:
        pl.when(cond)(act)


ME, MATE, CROSS, FAR = range(4)
NEAR = (ME, MATE)


def near(i, label):
    sign = 1 - 2 * (i % 2)
    return (i + (0, sign, 4 - sign, 2)[label]) % 4


def is_masked(lineage, a, b):
    return (b, a)[lineage] in NEAR


def arrange():
    stages = (
        ((ME, ME),),
        ((MATE, ME), (CROSS, ME), (FAR, ME)),
        ((ME, MATE), (ME, CROSS), (ME, FAR)),
        ((MATE, MATE), (MATE, CROSS), (MATE, FAR)),
        ((CROSS, MATE), (CROSS, CROSS), (CROSS, FAR)),
        ((FAR, MATE), (FAR, CROSS), (FAR, FAR)),
    )
    labels, bounds = [], []
    for stage in stages:
        both = [(lineage, a, b) for lineage in range(2) for a, b in stage]
        free = [(*label, part) for label in both[::-1] if not is_masked(*label) for part in range(2)]
        masked = [(*label, part) for part in range(2) for label in both if is_masked(*label)]
        start = len(labels)
        labels += free + masked
        bounds.append((start, start + len(free), start + len(free) + len(masked) // 2, len(labels)))
    return labels, bounds


LABELS, BOUNDS = arrange()
PLACE = {label: place for place, label in enumerate(LABELS)}


def kernel(
    hidden, w_down, gain, q_latent, q_rope, w_value, freq, out,
    hid_v, wd_v, ql_v, qr_v, wv_v, partial, sums, pieces, keys, q_f32, queries, cos_t, sin_t, acc, top, total,
    load_sem, rs_s, rs_r, z_s, z_r, a_s, a_r, b_s, b_r, c_s, c_r,
):
    seq = lax.axis_index("seq")
    tp = lax.axis_index("tp")
    core = seq % 2
    z = (seq // 2) % 8
    y_hi = seq // 16
    x = tp // 2
    y_lo = tp % 2
    y = y_hi * 2 + y_lo

    def device(x_, y_, z_):
        return (((y_ // 2) * 8 + z_) * 2 + core, x_ * 2 + y_ % 2)

    a_me = x * (1 - core) + y * core
    b_me = y * (1 - core) + x * core

    def plane(a_, b_):
        return device(a_ * (1 - core) + b_ * core, b_ * (1 - core) + a_ * core, z)

    sibling = (seq + 1 - 2 * core, tp)

    loads = [
        pltpu.make_async_copy(src, dst, load_sem.at[i])
        for i, (src, dst) in enumerate(
            ((hidden, hid_v), (w_down, wd_v), (q_rope, qr_v), (q_latent, ql_v), (w_value, wv_v))
        )
    ]
    for load in loads:
        load.start()

    barrier = pltpu.get_barrier_semaphore()
    peers = [(seq, (tp + d) % TP) for d in range(1, TP)]
    peers += [device(x, y, (z + d) % 8) for d in range(1, 8)]
    peers += [sibling, device(x, 3 - y, z), device(x, (y + 2) % 4, z)]
    for peer in peers:
        pl.semaphore_signal(barrier, inc=1, device_id=peer, device_id_type=MESH)

    loads[0].wait()
    loads[1].wait()
    partial[...] = dot(hid_v[...], wd_v[...], NT)
    pl.semaphore_wait(barrier, len(peers))

    sent = []

    def copy(src, dst, send_sem, recv_sem, target):
        return pltpu.make_async_remote_copy(
            src_ref=src, dst_ref=dst, send_sem=send_sem, recv_sem=recv_sem, device_id=target, device_id_type=MESH
        )

    def start(cond, *args):
        one = copy(*args)
        maybe(cond, one.start)
        sent.append((cond, one))

    def rows_of(owner):
        return partial.at[pl.ds(pl.multiple_of(owner * SLICE, SLICE), SLICE), :]

    for d in range(1, TP):
        owner = (tp + d) % TP
        start(True, rows_of(owner), sums.at[d], rs_s.at[d], rs_r.at[d], (seq, owner))

    positions = (seq * TOK + lax.broadcasted_iota(jnp.int32, (TOK, 128), 0)).astype(jnp.float32)
    angles = positions * freq[...]
    lane = lax.broadcasted_iota(jnp.int32, (1, 128), 1)
    cos_t[...] = jnp.cos(angles)
    sin_t[...] = jnp.where(lane % ROPE < ROPE // 2, -jnp.sin(angles), jnp.sin(angles))
    loads[2].wait()
    raw = qr_v[...].astype(jnp.float32)
    wide_lane = lax.broadcasted_iota(jnp.int32, (1, HEADS * ROPE), 1)
    swapped = jnp.where(
        wide_lane % ROPE < ROPE // 2,
        pltpu.roll(raw, HEADS * ROPE - ROPE // 2, 1),
        pltpu.roll(raw, ROPE // 2, 1),
    )
    repeat = HEADS * ROPE // 128
    rotated = raw * jnp.concatenate([cos_t[...]] * repeat, 1) + swapped * jnp.concatenate([sin_t[...]] * repeat, 1)
    rotated = rotated.astype(jnp.bfloat16)
    loads[3].wait()
    for c in range(KV_RANK // 128):
        q_f32[c] = ql_v[:, c * 128:(c + 1) * 128].astype(jnp.float32)
    for h in range(HEADS):
        for c in range(KV_RANK // 128):
            queries[h * TOK:(h + 1) * TOK, c * 128:(c + 1) * 128] = q_f32[
                c, pl.ds(h, TOK, stride=HEADS), :
            ].astype(jnp.bfloat16)
        mine = rotated[:, h * ROPE:(h + 1) * ROPE]
        queries[h * TOK:(h + 1) * TOK, KV_RANK:] = jnp.concatenate([mine, mine], 1)

    for d in range(1, TP):
        copy(rows_of(tp), sums.at[d], rs_s.at[d], rs_r.at[d], (seq, tp)).wait_recv()
    mine = pl.ds(pl.multiple_of(tp * SLICE, SLICE), SLICE)
    projection = partial[mine, :]
    for d in range(1, TP):
        projection = projection + sums[d]
    latent = projection[:, :KV_RANK]
    mean_square = jnp.mean(latent * latent, axis=-1, keepdims=True)
    latent = latent * lax.rsqrt(mean_square + EPSILON) * gain[...]
    rope = projection[:, KV_RANK:]
    rope_swapped = jnp.concatenate([rope[:, ROPE // 2:], rope[:, :ROPE // 2]], 1)
    rope = rope * cos_t[mine, :ROPE] + rope_swapped * sin_t[mine, :ROPE]

    def unit_at(lineage, a, b, part):
        first, second = PLACE[0, a, b, part], PLACE[1, a, b, part]
        place = first + (second - first) * lineage
        return keys.at[place]

    def unit(a, b, part):
        return unit_at(core, a, b, part)

    own_place = [PLACE[0, ME, ME, part] + (PLACE[1, ME, ME, part] - PLACE[0, ME, ME, part]) * core for part in range(2)]

    def slot(z_):
        return pieces.at[z_]

    slot(z)[...] = jnp.concatenate([latent, rope], 1).astype(jnp.bfloat16)

    for d in (4, 3, 5, 2, 6, 1, 7):
        start(True, slot(z), slot(z), z_s.at[d], z_r.at[d], device(x, y, (z + d) % 8))
    for d in range(1, 8):
        there = slot((z - d) % 8)
        copy(there, there, z_s.at[d], z_r.at[d], sibling).wait_recv()
    for part in range(2):
        four = [pieces[part * 4 + i] for i in range(4)]
        for i in range(4):
            for c in range(KV_RANK // 128):
                keys[own_place[part], c * HALF + i * SLICE:c * HALF + (i + 1) * SLICE, :] = four[i][:, c * 128:(c + 1) * 128]
        for i in range(2):
            at = KV_RANK // 128 * HALF + i * SLICE
            keys[own_place[part], at:at + SLICE, :] = jnp.concatenate([four[i][:, KV_RANK:], four[i + 2][:, KV_RANK:]], 1)

    early, late, even, odd = y_hi == 0, y_hi == 1, core == 0, core == 1

    def needed(lineage_even, a, b):
        if a in NEAR and b in NEAR:
            return True
        if b in NEAR:
            return late | lineage_even
        if a in NEAR:
            return late | jnp.logical_not(lineage_even)
        return late

    full = early | (z >= 4)

    def both(one, two):
        return two if one is True else one if two is True else one & two

    def kept(part, lineage_even, a, b):
        if part == 0 or not (a in NEAR or b in NEAR):
            return True
        if a in NEAR and b in NEAR:
            return full
        return full | (jnp.logical_not(lineage_even) if b in NEAR else lineage_even)

    def send_a(a):
        cond = True if a == MATE else even | early
        for part in range(2):
            start(
                both(cond, kept(part, even, a, ME)), unit(ME, ME, part), unit(a, ME, part),
                a_s.at[a, part], a_r.at[a, part], plane(near(a_me, a), b_me),
            )

    def send_b(a, b):
        if b == MATE:
            cond = True if a in NEAR else even | late
        else:
            cond = (even & early) | odd if a in NEAR else (even & early) | (odd & late)
        for part in range(2):
            start(
                both(cond, kept(part, even, a, b)), unit(a, ME, part), unit(a, b, part),
                b_s.at[b, a, part], b_r.at[b, a, part], plane(a_me, near(b_me, b)),
            )

    def to_sibling(a, b):
        for part in range(2):
            start(
                both(needed(even, a, b), kept(part, even, a, b)), unit(a, b, part), unit(a, b, part),
                c_s.at[b, a, part], c_r.at[b, a, part], sibling,
            )

    def arrived(lineage, lineage_even, a, b, recv_sem):
        for part in range(2):
            ref = unit_at(lineage, a, b, part)
            one = copy(ref, ref, c_s.at[0, 0, 0], recv_sem.at[part], sibling)
            maybe(both(needed(lineage_even, a, b), kept(part, lineage_even, a, b)), one.wait_recv)

    def got_a(a):
        arrived(core, even, a, ME, a_r.at[a])

    def got_b(a, b):
        arrived(core, even, a, b, b_r.at[b, a])

    def got_sibling(*labels):
        for a, b in labels:
            arrived(1 - core, odd, a, b, c_r.at[b, a])

    row = lax.broadcasted_iota(jnp.int32, (HALF, TOK), 0)
    token = lax.broadcasted_iota(jnp.int32, (HALF, TOK), 1)
    ahead = (row // SLICE) * (2 * TOK) + row % SLICE - token

    def bias(place):
        lineage, a, b, part = LABELS[place]
        x_label, y_label = (a, b) if lineage == 0 else (b, a)
        base = (lineage - core - 2 * z + 8 * part) * TOK + (near(x, x_label) * 2 + near(y, y_label) % 2) * SLICE
        return jnp.concatenate([jnp.where(ahead + base <= 0, 0.0, -1e30)] * (HEADS // 2), 1)

    sides = [(lane < ROPE).astype(jnp.bfloat16), (lane >= ROPE).astype(jnp.bfloat16)]

    def attend(halves, begin, end, first=False):
        blocks = range(begin, end)
        rows = jnp.concatenate(
            [
                jnp.concatenate([keys[place, c * HALF:(c + 1) * HALF, :] for place in blocks], 0)
                for c in range(KV_RANK // 128)
            ],
            1,
        )
        pairs = [keys[place, KV_RANK // 128 * HALF:, :] for place in blocks]
        ropes = jnp.concatenate([side * pair for pair in pairs for side in sides], 0)
        wide_rows = jnp.concatenate([rows, ropes], 1)
        masked = [place for place in blocks if is_masked(*LABELS[place][:3])]
        low = (masked[0] - begin) * HALF if masked else 0
        high = (masked[-1] + 1 - begin) * HALF if masked else 0
        mask = jnp.concatenate([bias(place) for place in masked], 0) if masked else None
        cuts = [slice(half * ROWS // 2, (half + 1) * ROWS // 2) for half in halves]

        def scores_of(cut):
            scores = dot(wide_rows, queries[cut, :], NT)
            if masked:
                split = [scores[low:high] + mask]
                if low > 0:
                    split.insert(0, scores[:low])
                if high < scores.shape[0]:
                    split.append(scores[high:])
                scores = jnp.concatenate(split, 0)
            return scores

        def weights_of(cut, scores):
            new_top = jnp.max(scores, 0, keepdims=True)
            scale = None
            if not first:
                new_top = jnp.maximum(top[0:1, cut], new_top)
            shift = new_top * EXP_SCALE
            weights = jnp.exp2(scores * EXP_SCALE - shift)
            added = jnp.sum(weights, 0, keepdims=True)
            if first:
                total[0:1, cut] = added
            else:
                scale = jnp.exp2(top[0:1, cut] * EXP_SCALE - shift)
                total[0:1, cut] = total[0:1, cut] * scale + added
            top[0:1, cut] = new_top
            return weights.astype(jnp.bfloat16), scale

        all_scores = [scores_of(cut) for cut in cuts]
        all_weights = [weights_of(cut, scores) for cut, scores in zip(cuts, all_scores)]
        for cut, (weights, scale) in zip(cuts, all_weights):
            mixed = dot(rows, weights, TN)
            acc[:, cut] = mixed if first else acc[:, cut] * scale + mixed

    def chunk(stage, halves=(0, 1)):
        begin, masked_begin, masked_half, end = BOUNDS[stage]
        first = stage == 0
        if first:
            pl.when(full)(lambda: attend(halves, begin, end, first))
        else:
            pl.when(early)(lambda: attend(halves, masked_begin, end))
            pl.when(late & full)(lambda: attend(halves, begin, end))
        pl.when(jnp.logical_not(full))(lambda: attend(halves, begin, masked_half, first))

    away = (MATE, CROSS, FAR)

    def landed(a):
        for b in away:
            got_b(a, b)
            to_sibling(a, b)

    def shared(a):
        got_sibling(*((a, b) for b in away))

    order = (MATE, CROSS, FAR)
    for a in order:
        send_a(a)
    to_sibling(ME, ME)
    got_sibling((ME, ME))
    for b in order:
        send_b(ME, b)
    chunk(0)
    for a in away:
        got_a(a)
        for b in order:
            send_b(a, b)
        to_sibling(a, ME)
    got_sibling(*((a, ME) for a in away))
    landed(ME)
    chunk(1)
    shared(ME)
    landed(MATE)
    chunk(2)
    shared(MATE)
    chunk(3, (0,))
    landed(CROSS)
    chunk(3, (1,))
    shared(CROSS)
    chunk(4)
    landed(FAR)
    begin, masked_begin, masked_half, last = BOUNDS[5]
    middle = begin + 6

    def even_lineage():
        pl.when(early)(lambda: attend((0, 1), masked_begin, last))
        pl.when(late & full)(lambda: attend((0, 1), middle, last))
        pl.when(jnp.logical_not(full))(lambda: attend((0, 1), middle, masked_half))

    def odd_lineage():
        pl.when(late)(lambda: attend((0, 1), begin, middle))

    pl.when(even)(even_lineage)
    pl.when(odd)(odd_lineage)
    shared(FAR)
    pl.when(even)(odd_lineage)
    pl.when(odd)(even_lineage)


    loads[4].wait()
    mixed = (acc[...] * (1.0 / total[0:1, :])).astype(jnp.bfloat16)
    for h in range(HEADS):
        cut = slice(h * TOK, (h + 1) * TOK)
        out[:, h * V_DIM:(h + 1) * V_DIM] = dot(mixed[:, cut], wv_v[h], TN)
    for cond, one in sent:
        maybe(cond, one.wait_send)


def shards(hidden, w_kv_down, kv_gain, q_latent, q_rope, w_value):
    half = ROPE // 2
    frequency = (10000.0 ** (-np.arange(half, dtype=np.float64) * 2.0 / ROPE)).astype(np.float32)
    freq = jnp.asarray(np.tile(frequency, 4)[None, :])
    hbm = pl.BlockSpec(memory_space=pl.ANY)
    vmem = pl.BlockSpec(memory_space=pltpu.VMEM)
    bf16, f32 = jnp.bfloat16, jnp.float32
    dma = pltpu.SemaphoreType.DMA
    width = hidden.shape[1]
    attended = pl.pallas_call(
        kernel,
        name="latent_attention",
        out_shape=jax.ShapeDtypeStruct((TOK, HEADS * V_DIM), f32),
        in_specs=[hbm, hbm, vmem, hbm, hbm, hbm, vmem],
        out_specs=vmem,
        scratch_shapes=[
            pltpu.VMEM((TOK, width), bf16),
            pltpu.VMEM((WIDTH, width), bf16),
            pltpu.VMEM((ROWS, KV_RANK), bf16),
            pltpu.VMEM((TOK, HEADS * ROPE), bf16),
            pltpu.VMEM((HEADS, KV_RANK, V_DIM), bf16),
            pltpu.VMEM((TOK, WIDTH), f32),
            pltpu.VMEM((TP, SLICE, WIDTH), f32),
            pltpu.VMEM((8, SLICE, WIDTH), bf16),
            pltpu.VMEM((64, HALF // 2 * 9, 128), bf16),
            pltpu.VMEM((KV_RANK // 128, ROWS, 128), f32),
            pltpu.VMEM((ROWS, WIDTH + ROPE), bf16),
            pltpu.VMEM((TOK, 128), f32),
            pltpu.VMEM((TOK, 128), f32),
            pltpu.VMEM((KV_RANK, ROWS), f32),
            pltpu.VMEM((8, ROWS), f32),
            pltpu.VMEM((8, ROWS), f32),
            dma((5,)),
            dma((8,)), dma((8,)),
            dma((8,)), dma((8,)),
            dma((4, 2)), dma((4, 2)),
            dma((4, 4, 2)), dma((4, 4, 2)),
            dma((4, 4, 2)), dma((4, 4, 2)),
        ],
        compiler_params=pltpu.CompilerParams(
            collective_id=0, has_side_effects=True, vmem_limit_bytes=60 * 2**20
        ),
    )(
        hidden,
        w_kv_down.T,
        kv_gain[None, :],
        q_latent.reshape(ROWS, KV_RANK),
        q_rope,
        w_value,
        freq,
    )
    return attended.astype(bf16)


def solution(mesh):
    placed = (
        P("seq", "tp"),
        P("tp", None),
        P(),
        P("seq", "tp", None),
        P("seq", "tp"),
        P("tp", None, None),
    )
    return jax.shard_map(
        shards, mesh=mesh, in_specs=placed, out_specs=P("seq", "tp"), check_vma=False
    )
```
